32 devices in a mesh: section: 1, seq: 16 (over z, y, x), mp: 2 (over core).
Axes of the slice: x: 2, y: 2, z: 4, core: 2. Of those that a mesh axis runs over, the one named last changes fastest.
Arguments:
- hidden_in: bfloat16 [4096, 5376], P('seq'), may hold values from -30 to 30
- query_weight: bfloat16 [1, 5376, 2048], P('section', 'seq', 'mp'), may hold values from -0.078125 to 0.078125
- key_weight: bfloat16 [1, 5376, 1024], P('section', 'seq', 'mp'), may hold values from -0.078125 to 0.078125
- value_weight: bfloat16 [1, 5376, 1024], P('section', 'seq', 'mp'), may hold values from -0.078125 to 0.078125
- output_weight: bfloat16 [1, 2048, 5376], P('section', 'mp', 'seq'), may hold values from -0.5524272 to 0.5524272
- input_gain: bfloat16 [1, 5376], P('section'), may hold values from 0.099609375 to 1.8984375
- post_gain: bfloat16 [1, 5376], P('section', 'mp'), may hold values from 0.099609375 to 1.8984375
Outputs:
- hidden_out: bfloat16 [1, 4096, 5376], P('section', 'seq', 'mp')
The draws below stay inside these ranges and needn't reach their ends.
All inputs are finite; a program needn't handle non-finite values.
Results may differ from the reference program's by a relative error of at most 0.013.
Values may be sent and summed in bfloat16 or wider, within the bound.
A program may use at most 128 MiB of HBM per device.

```python
import math
import jax
import jax.numpy as jnp
from jax import lax

D = 5376
HEADS = 16
KV_HEADS = 8
HEAD_DIM = 128
WINDOW = 1024
QSCALE = 168
TOK_DEV = 256
TOKENS = 4096
LAYERS = 1
N_SEQ = 16
N_MP = 2


def draw_hidden_in(key, part):
    base_key, row_key, column_key = jax.random.split(key, 3)
    base_values = jnp.clip(jax.random.normal(base_key, (TOKENS, D), jnp.float32), -5.0, 5.0)
    column_low = 0.5
    column_high = 2.0
    row_scale = jnp.exp(jax.random.uniform(row_key, (TOKENS, 1), jnp.float32, math.log(0.3), math.log(3.0)))
    column_scale = jnp.exp(jax.random.uniform(column_key, (1, D), jnp.float32, math.log(column_low), math.log(column_high)))
    return (base_values * row_scale * column_scale).astype(jnp.bfloat16)


def draw_output_weight(key, part):
    base_key, jitter_key = jax.random.split(key, 2)
    fan_width = HEADS * HEAD_DIM
    rising = jnp.arange(D, dtype=jnp.float32) / D
    base_values = jnp.clip(jax.random.normal(base_key, (LAYERS, fan_width, D), jnp.float32), -5.0, 5.0)
    ramp = jnp.exp(rising * math.log(3.0))
    jitter = jnp.exp(jax.random.uniform(jitter_key, (LAYERS, 1, D), jnp.float32, math.log(0.7), math.log(1.4)))
    return (base_values / math.sqrt(fan_width) * ramp[None, None, :] * jitter).astype(jnp.bfloat16)


def levels(rng, shape, pieces, smallest, high):
    def one(position, blocks):
        draws = jax.random.uniform(jax.random.fold_in(jax.random.fold_in(rng, 6), position), (blocks,), jnp.float32, smallest / len(pieces), high / len(pieces))
        return jnp.repeat(jnp.exp(draws), shape[position] // blocks).reshape((-1,) + (1,) * (len(shape) - position - 1))

    level = one(*pieces[0])
    for cut in pieces[1:]:
        level = level * one(*cut)
    return level


def noise(own_key, dims, deviation, limit, pieces=(), held_as=jnp.bfloat16):
    factor_of = levels(own_key, dims, pieces, -0.22, 0.18) if pieces else 1.0
    values = jax.random.normal(own_key, dims, jnp.float32) * deviation * factor_of
    return jnp.minimum(jnp.maximum(values, -limit), limit).astype(held_as)


def setup_inputs(seed: int = 0) -> dict:
    keys = jax.random.split(jax.random.key(seed), 8)
    hidden_in = draw_hidden_in(jax.random.fold_in(keys[7], 71), 0)
    query_weight = noise(keys[1], (LAYERS, D, HEADS * HEAD_DIM), D ** -0.5, 0.078125, ((1, 16), (2, 2)))
    key_weight = noise(keys[2], (LAYERS, D, KV_HEADS * HEAD_DIM), D ** -0.5, 0.078125, ((1, 16), (2, 2)))
    value_weight = noise(keys[3], (LAYERS, D, KV_HEADS * HEAD_DIM), D ** -0.5, 0.078125, ((1, 16), (2, 2)))
    output_weight = draw_output_weight(jax.random.fold_in(keys[7], 71), 0)
    input_gain = jnp.clip(1.0 + 0.18 * jax.random.normal(keys[5], (LAYERS, D), jnp.float32), 0.099609375, 1.8984375).astype(jnp.bfloat16)
    post_gain = jnp.clip(1.0 + 0.18 * jax.random.normal(keys[6], (LAYERS, D), jnp.float32), 0.099609375, 1.8984375).astype(jnp.bfloat16)
    return dict(hidden_in=hidden_in, query_weight=query_weight, key_weight=key_weight, value_weight=value_weight, output_weight=output_weight, input_gain=input_gain, post_gain=post_gain)


NORM_EPS = 1e-06

def rope_tables(positions, head_size):
    half_dim = head_size // 2
    frequency = jnp.exp(-math.log(10000.0) * (2.0 * jnp.arange(half_dim, dtype=jnp.float32)) / head_size)
    angles = positions.astype(jnp.float32)[:, None] * frequency[None, :]
    return (jnp.cos(angles), jnp.sin(angles))

def norm_rotate(values, cosine, sine_table):
    scaled = values * lax.rsqrt(lax.optimization_barrier(jnp.mean(values * values, axis=-1, keepdims=True)) + NORM_EPS)
    half_dim = scaled.shape[-1] // 2
    leading = scaled[..., :half_dim]
    trailing = scaled[..., half_dim:]
    cosine = cosine[:, None, :]
    sine_table = sine_table[:, None, :]
    rotated = jnp.concatenate([leading * cosine - trailing * sine_table, trailing * cosine + leading * sine_table], axis=-1)
    return rotated.astype(jnp.bfloat16)

def attend_layer(hidden, query_weight, key_weight, value_weight, output_weight, input_gain, post_gain):
    rows_float = hidden.astype(jnp.float32)
    normed = (rows_float * lax.rsqrt(lax.optimization_barrier(jnp.mean(rows_float * rows_float, axis=1, keepdims=True)) + NORM_EPS) * input_gain.astype(jnp.float32)).astype(jnp.bfloat16)
    queries = jnp.dot(normed, query_weight, preferred_element_type=jnp.float32)
    keys_raw = jnp.dot(normed, key_weight, preferred_element_type=jnp.float32)
    values_raw = jnp.dot(normed, value_weight, preferred_element_type=jnp.float32)
    positions = jnp.arange(TOKENS, dtype=jnp.int32)
    cosine, sine_table = rope_tables(positions, HEAD_DIM)
    query_heads = norm_rotate(queries.reshape(TOKENS, HEADS, HEAD_DIM), cosine, sine_table)
    key_heads = norm_rotate(keys_raw.reshape(TOKENS, KV_HEADS, HEAD_DIM), cosine, sine_table)
    value_heads = values_raw.astype(jnp.bfloat16).reshape(TOKENS, KV_HEADS, HEAD_DIM)
    reach_shards = (WINDOW + TOK_DEV - 2) // TOK_DEV
    margin = reach_shards * TOK_DEV
    key_padded = jnp.concatenate([jnp.zeros((margin, KV_HEADS, HEAD_DIM), jnp.bfloat16), key_heads], axis=0)
    value_padded = jnp.concatenate([jnp.zeros((margin, KV_HEADS, HEAD_DIM), jnp.bfloat16), value_heads], axis=0)
    group_size = HEADS // KV_HEADS
    window_count = margin + TOK_DEV
    score_scale = 1.0 / math.sqrt(QSCALE)

    def one_block(block_index):
        start = (block_index * TOK_DEV).astype(jnp.int32)
        query_block = lax.dynamic_slice_in_dim(query_heads, start, TOK_DEV, 0).astype(jnp.float32)
        query_block = query_block.reshape(TOK_DEV, KV_HEADS, group_size, HEAD_DIM)
        key_block = lax.dynamic_slice_in_dim(key_padded, start, window_count, 0).astype(jnp.float32)
        value_block = lax.dynamic_slice_in_dim(value_padded, start, window_count, 0).astype(jnp.float32)
        query_pos = start + jnp.arange(TOK_DEV, dtype=jnp.int32)
        key_pos = start - margin + jnp.arange(window_count, dtype=jnp.int32)
        distance = query_pos[:, None] - key_pos[None, :]
        visible = ((distance >= 0) & (distance < WINDOW) & (key_pos[None, :] >= 0)).astype(jnp.float32)
        scores = jnp.einsum('tkgd,skd->kgts', query_block, key_block) * score_scale
        weights_raw = jnp.exp(scores) * visible
        softmax_weights = (weights_raw / lax.optimization_barrier(jnp.sum(weights_raw, axis=-1, keepdims=True))).astype(jnp.bfloat16)
        softmax_weights = lax.optimization_barrier(softmax_weights).astype(jnp.float32)
        attended = jnp.einsum('kgts,skd->tkgd', softmax_weights, value_block).astype(jnp.bfloat16)
        return attended.reshape(TOK_DEV, HEADS * HEAD_DIM)
    attended = lax.map(one_block, jnp.arange(N_SEQ, dtype=jnp.int32)).reshape(TOKENS, HEADS * HEAD_DIM)
    core_columns = HEADS // N_MP * HEAD_DIM
    mixed = jnp.zeros((TOKENS, D), jnp.float32)
    for core_index in range(N_MP):
        partial_value = jnp.dot(attended[:, core_index * core_columns:(core_index + 1) * core_columns], output_weight[core_index * core_columns:(core_index + 1) * core_columns], preferred_element_type=jnp.float32)
        mixed = mixed + lax.optimization_barrier(partial_value.astype(jnp.bfloat16)).astype(jnp.float32)
    branch = mixed * lax.rsqrt(lax.optimization_barrier(jnp.mean(mixed * mixed, axis=1, keepdims=True)) + NORM_EPS) * post_gain.astype(jnp.float32)
    return (rows_float + branch).astype(jnp.bfloat16)

def reference(hidden_in, query_weight, key_weight, value_weight, output_weight, input_gain, post_gain):
    outputs = []
    current = hidden_in
    for layer_index in range(LAYERS):
        current = attend_layer(current, query_weight[layer_index], key_weight[layer_index], value_weight[layer_index], output_weight[layer_index], input_gain[layer_index], post_gain[layer_index])
        outputs.append(current)
    return jnp.stack(outputs)
```

```python
import functools
import math

import jax
import jax.numpy as jnp
from jax import lax
from jax.experimental import pallas as pl
from jax.experimental.pallas import tpu as pltpu
from jax.sharding import PartitionSpec as P

HEADS = 16
KV_HEADS = 8
HEAD_DIM = 128
WINDOW = 1024
QSCALE = 168


NORM_EPS = 1e-06
MESH = pl.DeviceIdType.MESH


def from_behind(block, axis, distance):
    devices = range(lax.axis_size(axis))
    route = [(i - distance, i) for i in devices if i - distance in devices]
    return lax.ppermute(block, axis, route)


def rope_tables(positions, head_size):
    half_dim = head_size // 2
    frequency = jnp.exp(
        -math.log(10000.0) * (2.0 * jnp.arange(half_dim, dtype=jnp.float32)) / head_size
    )
    angles = positions.astype(jnp.float32)[:, None] * frequency[None, :]
    return (jnp.cos(angles), jnp.sin(angles))


def place(group_size):
    shard = lax.axis_index("seq")
    return lax.div(shard, group_size), lax.rem(shard, group_size), lax.axis_index("mp")


def gather_kernel(
    groups, group_size, rows_ref, query_ref, key_ref, value_ref,
    weights_ref, tokens_ref,
    own_sem, plane_send, plane_recv, token_send, token_recv, twin_send, twin_recv,
    up_send, up_recv, down_send, down_recv,
):
    group, member, core = place(group_size)
    here = group * group_size
    shard = here + member
    barrier = pltpu.get_barrier_semaphore()
    for d in range(1, group_size):
        peer = here + lax.rem(member + d, group_size)
        pl.semaphore_signal(barrier, inc=1, device_id={"seq": peer}, device_id_type=MESH)
    pl.semaphore_signal(barrier, inc=1, device_id={"mp": 1 - core}, device_id_type=MESH)
    above = shard + group_size
    below = shard - group_size

    @pl.when(group > 0)
    def _():
        pl.semaphore_signal(barrier, inc=1, device_id={"seq": below}, device_id_type=MESH)

    @pl.when(group < groups - 1)
    def _():
        pl.semaphore_signal(barrier, inc=1, device_id={"seq": above}, device_id_type=MESH)

    pl.semaphore_wait(
        barrier,
        group_size + jnp.where(group > 0, 1, 0) + jnp.where(group < groups - 1, 1, 0),
    )

    sources = (query_ref, key_ref, value_ref)
    widths = [ref.shape[1] // group_size for ref in sources]
    starts = [0, widths[0], widths[0] + widths[1]]

    def piece(part, index):
        width = widths[part]
        return sources[part].at[:, pl.ds(pl.multiple_of(index * width, width), width)]

    def slot(block, part):
        return weights_ref.at[block, :, pl.ds(starts[part], widths[part])]

    own = [
        pltpu.make_async_copy(piece(part, member), slot(shard, part), own_sem.at[part])
        for part in range(3)
    ]
    for copy in own:
        copy.start()
    plane = []
    for d in range(1, group_size):
        index = lax.rem(member + d, group_size)
        for part in range(3):
            copy = pltpu.make_async_remote_copy(
                src_ref=piece(part, index),
                dst_ref=slot(shard, part),
                send_sem=plane_send.at[d - 1, part],
                recv_sem=plane_recv.at[d - 1, part],
                device_id={"seq": here + index},
                device_id_type=MESH,
            )
            copy.start()
            plane.append(copy)
    own_rows = pltpu.make_async_copy(rows_ref, tokens_ref.at[member], own_sem.at[3])
    own_rows.start()
    token_copies = []
    for d in range(1, group_size):
        index = lax.rem(member + d, group_size)
        copy = pltpu.make_async_remote_copy(
            src_ref=rows_ref.at[core],
            dst_ref=tokens_ref.at[member, core],
            send_sem=token_send.at[d - 1],
            recv_sem=token_recv.at[d - 1],
            device_id={"seq": here + index},
            device_id_type=MESH,
        )
        copy.start()
        token_copies.append(copy)

    def relay(step, d, upward):
        origin = group - step + 1 if upward else group + step - 1
        block = origin * group_size + lax.rem(member - d + group_size, group_size)
        send, recv = (up_send, up_recv) if upward else (down_send, down_recv)
        return pltpu.make_async_remote_copy(
            src_ref=weights_ref.at[block],
            dst_ref=weights_ref.at[block],
            send_sem=send.at[step - 1, d],
            recv_sem=recv.at[step - 1, d],
            device_id={"seq": above if upward else below},
            device_id_type=MESH,
        )

    def arrival(step, d, upward):
        origin = group - step if upward else group + step
        block = origin * group_size + lax.rem(member - d + group_size, group_size)
        send, recv = (up_send, up_recv) if upward else (down_send, down_recv)
        return pltpu.make_async_remote_copy(
            src_ref=weights_ref.at[block],
            dst_ref=weights_ref.at[block],
            send_sem=send.at[step - 1, d],
            recv_sem=recv.at[step - 1, d],
            device_id={"seq": above if upward else below},
            device_id_type=MESH,
        )

    def sends(step, upward):
        if upward:
            return (group < groups - 1) & (group - step + 1 >= 0)
        return (group > 0) & (group + step - 1 <= groups - 1)

    def receives(step, upward):
        return group - step >= 0 if upward else group + step <= groups - 1

    twins = []
    for step in range(1, groups):
        for d in range(group_size):
            if step == 1:
                if d == 0:
                    for copy in own:
                        copy.wait()
                else:
                    for part in range(3):
                        origin = here + lax.rem(member - d + group_size, group_size)
                        pltpu.make_async_remote_copy(
                            src_ref=piece(part, member),
                            dst_ref=slot(origin, part),
                            send_sem=plane_send.at[d - 1, part],
                            recv_sem=plane_recv.at[d - 1, part],
                            device_id={"seq": origin},
                            device_id_type=MESH,
                        ).wait_recv()
            for upward in (True, False):
                if step > 1:

                    @pl.when(receives(step - 1, upward))
                    def _():
                        arrival(step - 1, d, upward).wait_recv()

                @pl.when(sends(step, upward))
                def _():
                    relay(step, d, upward).start()

        if step == 1:
            for d in range(1, group_size):
                origin = lax.rem(member - d + group_size, group_size)
                pltpu.make_async_remote_copy(
                    src_ref=rows_ref.at[core],
                    dst_ref=tokens_ref.at[origin, core],
                    send_sem=token_send.at[d - 1],
                    recv_sem=token_recv.at[d - 1],
                    device_id={"seq": here + origin},
                    device_id_type=MESH,
                ).wait_recv()
                copy = pltpu.make_async_remote_copy(
                    src_ref=tokens_ref.at[origin, core],
                    dst_ref=tokens_ref.at[origin, core],
                    send_sem=twin_send.at[d - 1],
                    recv_sem=twin_recv.at[d - 1],
                    device_id={"mp": 1 - core},
                    device_id_type=MESH,
                )
                copy.start()
                twins.append(copy)

    own_rows.wait()
    for copy in plane + token_copies:
        copy.wait_send()
    for d in range(1, group_size):
        origin = lax.rem(member - d + group_size, group_size)
        twins[d - 1].wait_send()
        pltpu.make_async_remote_copy(
            src_ref=tokens_ref.at[origin, 1 - core],
            dst_ref=tokens_ref.at[origin, 1 - core],
            send_sem=twin_send.at[d - 1],
            recv_sem=twin_recv.at[d - 1],
            device_id={"mp": 1 - core},
            device_id_type=MESH,
        ).wait_recv()
    for step in range(1, groups):
        for d in range(group_size):
            for upward in (True, False):

                @pl.when(sends(step, upward))
                def _():
                    relay(step, d, upward).wait_send()

                if step == groups - 1:

                    @pl.when(receives(step, upward))
                    def _():
                        arrival(step, d, upward).wait_recv()


def gather(rows, query_weight, key_weight, value_weight, group_size):
    shards = lax.axis_size("seq")
    groups = shards // group_size
    depth = query_weight.shape[0]
    width = (query_weight.shape[1] + key_weight.shape[1] + value_weight.shape[1]) // group_size
    row_count, model_width = rows.shape
    halves = rows.reshape(2, row_count // 2, model_width)
    dma = pltpu.SemaphoreType.DMA
    anywhere = pl.BlockSpec(memory_space=pl.ANY)
    weights, tokens = pl.pallas_call(
        functools.partial(gather_kernel, groups, group_size),
        out_shape=(
            jax.ShapeDtypeStruct((shards, depth, width), jnp.bfloat16),
            jax.ShapeDtypeStruct((group_size,) + halves.shape, jnp.bfloat16),
        ),
        in_specs=[anywhere] * 4,
        out_specs=(anywhere, anywhere),
        scratch_shapes=[
            dma((4,)),
            dma((group_size - 1, 3)),
            dma((group_size - 1, 3)),
            dma((group_size - 1,)),
            dma((group_size - 1,)),
            dma((group_size - 1,)),
            dma((group_size - 1,)),
            dma((groups - 1, group_size)),
            dma((groups - 1, group_size)),
            dma((groups - 1, group_size)),
            dma((groups - 1, group_size)),
        ],
        compiler_params=pltpu.CompilerParams(collective_id=0, has_side_effects=True),
        name="gather",
    )(halves, query_weight, key_weight, value_weight)
    return weights.reshape(shards * depth, width), tokens.reshape(-1, model_width)


def attend_kernel(
    groups, group_size, row_count, projected_ref, cosine_ref, sine_ref, out_ref,
    query_ref, window_ref, sent_ref, halo_send, halo_recv, send_sem, recv_sem,
):
    group, member, core = place(group_size)
    here = group * group_size
    shard = here + member
    above = shard + group_size
    below = shard - group_size
    barrier = pltpu.get_barrier_semaphore()
    for d in range(1, group_size):
        peer = here + lax.rem(member + d, group_size)
        pl.semaphore_signal(barrier, inc=1, device_id={"seq": peer}, device_id_type=MESH)

    @pl.when(group > 0)
    def _():
        pl.semaphore_signal(barrier, inc=1, device_id={"seq": below}, device_id_type=MESH)

    @pl.when(group < groups - 1)
    def _():
        pl.semaphore_signal(barrier, inc=1, device_id={"seq": above}, device_id_type=MESH)

    pl.semaphore_wait(
        barrier,
        group_size - 1 + jnp.where(group > 0, 1, 0) + jnp.where(group < groups - 1, 1, 0),
    )
    span = group_size * row_count
    query_width = query_ref.shape[1]
    query_heads = query_width // HEAD_DIM

    def rotated(block):
        scaled = block * lax.rsqrt(jnp.mean(block * block, axis=-1, keepdims=True) + NORM_EPS)
        turned = pltpu.roll(scaled, HEAD_DIM // 2, 1)
        return (scaled * cosine_ref[...] + turned * sine_ref[...]).astype(jnp.bfloat16)

    window_ref[pl.ds(span, span), :HEAD_DIM] = rotated(
        projected_ref[:, query_width : query_width + HEAD_DIM]
    )
    window_ref[pl.ds(span, span), HEAD_DIM:] = projected_ref[
        :, query_width + HEAD_DIM :
    ].astype(jnp.bfloat16)
    halo = pltpu.make_async_remote_copy(
        src_ref=window_ref.at[pl.ds(span, span)],
        dst_ref=window_ref.at[pl.ds(0, span)],
        send_sem=halo_send,
        recv_sem=halo_recv,
        device_id={"seq": above},
        device_id_type=MESH,
    )

    @pl.when(group < groups - 1)
    def _():
        halo.start()

    for head in range(query_heads):
        columns = slice(head * HEAD_DIM, (head + 1) * HEAD_DIM)
        query_ref[:, columns] = rotated(projected_ref[:, columns])

    @pl.when(group == 0)
    def _():
        window_ref[pl.ds(0, span), :] = jnp.zeros((span, window_ref.shape[1]), jnp.bfloat16)

    @pl.when(group > 0)
    def _():
        halo.wait_recv()

    reach = span + row_count
    query_pos = lax.broadcasted_iota(jnp.int32, (row_count, reach), 0) + span
    key_pos = lax.broadcasted_iota(jnp.int32, (row_count, reach), 1)
    distance = query_pos - key_pos
    near = (distance >= 0) & (distance < WINDOW)
    score_scale = 1.0 / math.sqrt(QSCALE)
    copies = []
    for turn in range(1, group_size + 1):
        index = lax.rem(member + turn, group_size)
        first = pl.multiple_of(index * row_count, row_count)
        keys = window_ref[pl.ds(first, reach), :HEAD_DIM]
        values = window_ref[pl.ds(first, reach), HEAD_DIM:]
        visible = near & (key_pos + first + group * span >= span)
        for head in range(query_heads):
            columns = slice(head * HEAD_DIM, (head + 1) * HEAD_DIM)
            scores = lax.dot_general(
                query_ref[pl.ds(first, row_count), columns], keys,
                (((1,), (1,)), ((), ())), preferred_element_type=jnp.float32,
            )
            raw = jnp.where(visible, jnp.exp(scores * score_scale), 0.0)
            probs = (raw * (1.0 / jnp.sum(raw, axis=-1, keepdims=True))).astype(jnp.bfloat16)
            sent_ref[turn - 1, :, columns] = jnp.dot(
                probs, values, preferred_element_type=jnp.float32
            ).astype(jnp.bfloat16)
        mine = out_ref.at[:, pl.ds(pl.multiple_of(member * query_width, query_width), query_width)]
        if turn < group_size:
            copy = pltpu.make_async_remote_copy(
                src_ref=sent_ref.at[turn - 1],
                dst_ref=mine,
                send_sem=send_sem.at[turn - 1],
                recv_sem=recv_sem.at[turn - 1],
                device_id={"seq": here + index},
                device_id_type=MESH,
            )
        else:
            copy = pltpu.make_async_copy(sent_ref.at[turn - 1], mine, send_sem.at[turn - 1])
        copy.start()
        copies.append(copy)
    copies[-1].wait()
    for turn in range(1, group_size):
        copies[turn - 1].wait_send()
        origin = lax.rem(member - turn + group_size, group_size)
        pltpu.make_async_remote_copy(
            src_ref=sent_ref.at[turn - 1],
            dst_ref=out_ref.at[
                :, pl.ds(pl.multiple_of(origin * query_width, query_width), query_width)
            ],
            send_sem=send_sem.at[turn - 1],
            recv_sem=recv_sem.at[turn - 1],
            device_id={"seq": here + origin},
            device_id_type=MESH,
        ).wait_recv()

    @pl.when(group < groups - 1)
    def _():
        halo.wait_send()


def attend(projected, cosine, sine, group_size):
    groups = lax.axis_size("seq") // group_size
    span = projected.shape[0]
    row_count = span // group_size
    query_width = projected.shape[1] - 2 * HEAD_DIM
    dma = pltpu.SemaphoreType.DMA
    vmem = pl.BlockSpec(memory_space=pltpu.VMEM)
    return pl.pallas_call(
        functools.partial(attend_kernel, groups, group_size, row_count),
        out_shape=jax.ShapeDtypeStruct((row_count, group_size * query_width), jnp.bfloat16),
        in_specs=[vmem] * 3,
        out_specs=vmem,
        scratch_shapes=[
            pltpu.VMEM((span, query_width), jnp.bfloat16),
            pltpu.VMEM((2 * span, 2 * HEAD_DIM), jnp.bfloat16),
            pltpu.VMEM((group_size, row_count, query_width), jnp.bfloat16),
            dma,
            dma,
            dma((group_size,)),
            dma((group_size - 1,)),
        ],
        compiler_params=pltpu.CompilerParams(
            collective_id=1, has_side_effects=True, vmem_limit_bytes=40 * 1024 * 1024
        ),
        name="attend",
    )(projected, cosine, sine)


def body(hidden_in, query_weight, key_weight, value_weight, output_weight, input_gain, post_gain):
    row_count, model_width = hidden_in.shape
    half_width = post_gain.shape[1]
    core_index = lax.axis_index("mp")
    shard_index = lax.axis_index("seq")
    section_index = lax.axis_index("section")
    sections = lax.axis_size("section")
    shards = lax.axis_size("seq")
    group_size = key_weight.shape[2] // HEAD_DIM
    gain_first = input_gain[0].astype(jnp.float32)
    gain_second = post_gain[0].astype(jnp.float32)
    output_full = lax.all_gather(output_weight[0], "seq", axis=1, tiled=True)
    span = group_size * row_count
    positions = (shard_index // group_size) * span + jnp.arange(span, dtype=jnp.int32)
    cosine, sine = rope_tables(positions, HEAD_DIM)
    cosine = jnp.concatenate([cosine, cosine], axis=1)
    sine = jnp.concatenate([-sine, sine], axis=1)

    def normed_rows(full_rows):
        rows_float = full_rows.astype(jnp.float32)
        return (
            rows_float
            * lax.rsqrt(jnp.mean(rows_float * rows_float, axis=1, keepdims=True) + NORM_EPS)
            * gain_first
        ).astype(jnp.bfloat16)

    def attend_layer(weights, tokens, residual_half):
        projected = jnp.dot(tokens, weights, preferred_element_type=jnp.float32)
        attended = attend(projected, cosine, sine, group_size)
        partial_value = jnp.dot(attended, output_full, preferred_element_type=jnp.float32)
        summed = lax.psum_scatter(
            partial_value.astype(jnp.bfloat16), "mp", scatter_dimension=1, tiled=True
        ).astype(jnp.float32)
        squares = lax.psum(jnp.sum(summed * summed, axis=1, keepdims=True), "mp")
        branch = summed * lax.rsqrt(squares / model_width + NORM_EPS) * gain_second
        return (residual_half.astype(jnp.float32) + branch).astype(jnp.bfloat16)

    own_half = lax.dynamic_slice_in_dim(hidden_in, core_index * half_width, half_width, 1)
    weights, tokens = gather(
        normed_rows(hidden_in), query_weight[0], key_weight[0], value_weight[0], group_size
    )
    layer = attend_layer(weights, tokens, own_half)
    result = layer
    plane = [
        list(range(first, first + group_size)) for first in range(0, shards, group_size)
    ]
    for step in range(1, sections):
        arrived = from_behind(layer, "section", 1)
        rows = normed_rows(lax.all_gather(arrived, "mp", axis=1, tiled=True))
        tokens = lax.all_gather(rows, "seq", axis=0, tiled=True, axis_index_groups=plane)
        layer = attend_layer(weights, tokens, arrived)
        result = jnp.where(section_index == step, layer, result)
    return result[None]


def solution(mesh):
    placed = (
        P("seq", None),
        P("section", "seq", "mp"),
        P("section", "seq", "mp"),
        P("section", "seq", "mp"),
        P("section", "mp", "seq"),
        P("section", None),
        P("section", "mp"),
    )
    return jax.shard_map(
        body, mesh=mesh, in_specs=placed, out_specs=P("section", "seq", "mp"), check_vma=False
    )
```

```python
import functools
import math

import jax
import jax.numpy as jnp
from jax import lax
from jax.experimental import pallas as pl
from jax.experimental.pallas import tpu as pltpu
from jax.sharding import PartitionSpec as P

HEADS = 16
KV_HEADS = 8
HEAD_DIM = 128
WINDOW = 1024
QSCALE = 168


NORM_EPS = 1e-06
MESH = pl.DeviceIdType.MESH


def from_behind(block, axis, distance):
    devices = range(lax.axis_size(axis))
    route = [(i - distance, i) for i in devices if i - distance in devices]
    return lax.ppermute(block, axis, route)


def rope_tables(positions, head_size):
    half_dim = head_size // 2
    frequency = jnp.exp(
        -math.log(10000.0) * (2.0 * jnp.arange(half_dim, dtype=jnp.float32)) / head_size
    )
    angles = positions.astype(jnp.float32)[:, None] * frequency[None, :]
    return (jnp.cos(angles), jnp.sin(angles))


def place(group_size):
    shard = lax.axis_index("seq")
    return lax.div(shard, group_size), lax.rem(shard, group_size), lax.axis_index("mp")


def gather_kernel(
    groups, group_size, rows_ref, query_ref, key_ref, value_ref, mix_ref,
    weights_ref, tokens_ref, mixes_ref,
    own_sem, plane_send, plane_recv, token_send, token_recv, twin_send, twin_recv,
    up_send, up_recv, down_send, down_recv,
    side_send, side_recv, pass_send, pass_recv,
):
    group, member, core = place(group_size)
    here = group * group_size
    shard = here + member
    barrier = pltpu.get_barrier_semaphore()
    for d in range(1, group_size):
        peer = here + lax.rem(member + d, group_size)
        pl.semaphore_signal(barrier, inc=1, device_id={"seq": peer}, device_id_type=MESH)
    pl.semaphore_signal(barrier, inc=1, device_id={"mp": 1 - core}, device_id_type=MESH)
    above = shard + group_size
    below = shard - group_size

    @pl.when(group > 0)
    def _():
        pl.semaphore_signal(barrier, inc=1, device_id={"seq": below}, device_id_type=MESH)

    @pl.when(group < groups - 1)
    def _():
        pl.semaphore_signal(barrier, inc=1, device_id={"seq": above}, device_id_type=MESH)

    pl.semaphore_wait(
        barrier,
        group_size + jnp.where(group > 0, 1, 0) + jnp.where(group < groups - 1, 1, 0),
    )

    sources = (query_ref, key_ref, value_ref)
    widths = [ref.shape[1] // group_size for ref in sources]
    starts = [0, widths[0], widths[0] + widths[1]]

    def piece(part, index):
        width = widths[part]
        return sources[part].at[:, pl.ds(pl.multiple_of(index * width, width), width)]

    def slot(block, part):
        return weights_ref.at[block, :, pl.ds(starts[part], widths[part])]

    own = [
        pltpu.make_async_copy(piece(part, member), slot(shard, part), own_sem.at[part])
        for part in range(3)
    ]
    for copy in own:
        copy.start()
    plane = []
    for d in range(1, group_size):
        index = lax.rem(member + d, group_size)
        for part in range(3):
            copy = pltpu.make_async_remote_copy(
                src_ref=piece(part, index),
                dst_ref=slot(shard, part),
                send_sem=plane_send.at[d - 1, part],
                recv_sem=plane_recv.at[d - 1, part],
                device_id={"seq": here + index},
                device_id_type=MESH,
            )
            copy.start()
            plane.append(copy)
    own_rows = pltpu.make_async_copy(rows_ref, tokens_ref.at[member], own_sem.at[3])
    own_rows.start()
    own_mix = pltpu.make_async_copy(mix_ref, mixes_ref.at[shard], own_sem.at[4])
    own_mix.start()

    def flipped(bits):
        low = lax.rem(member, 2)
        high = member - low
        if bits & 1:
            low = 1 - low
        if bits & 2:
            high = 2 - high
        return high + low

    half_columns = rows_ref.shape[2] // 2

    def token_direct(bits, sender):
        return pltpu.make_async_remote_copy(
            src_ref=rows_ref.at[core],
            dst_ref=tokens_ref.at[sender, core],
            send_sem=token_send.at[bits - 1],
            recv_sem=token_recv.at[bits - 1],
            device_id={"seq": here + flipped(bits)},
            device_id_type=MESH,
        )

    def token_half(owner, which, bits):
        part = tokens_ref.at[owner, core, :, pl.ds(which * half_columns, half_columns)]
        return pltpu.make_async_remote_copy(
            src_ref=part,
            dst_ref=part,
            send_sem=token_send.at[2 + which],
            recv_sem=token_recv.at[2 + which],
            device_id={"seq": here + flipped(bits)},
            device_id_type=MESH,
        )

    def twin(index, half):
        if index < 2:
            part = tokens_ref.at[flipped(index + 1), half]
        else:
            part = tokens_ref.at[
                flipped(3), half, :, pl.ds((index - 2) * half_columns, half_columns)
            ]
        return pltpu.make_async_remote_copy(
            src_ref=part,
            dst_ref=part,
            send_sem=twin_send.at[index],
            recv_sem=twin_recv.at[index],
            device_id={"mp": 1 - core},
            device_id_type=MESH,
        )

    token_direct(1, member).start()
    token_direct(2, member).start()

    mix_half = mix_ref.shape[1] // 2

    def mix_side(origin, bits, owner, own):
        block = mixes_ref.at[origin * group_size + owner]
        return pltpu.make_async_remote_copy(
            src_ref=mix_ref if own else block,
            dst_ref=block,
            send_sem=side_send.at[bits - 1, origin],
            recv_sem=side_recv.at[bits - 1, origin],
            device_id={"seq": here + flipped(bits)},
            device_id_type=MESH,
        )

    def mix_pass(origin, owner, which, bits):
        part = mixes_ref.at[
            origin * group_size + owner, :, pl.ds(which * mix_half, mix_half)
        ]
        return pltpu.make_async_remote_copy(
            src_ref=part,
            dst_ref=part,
            send_sem=pass_send.at[which, origin],
            recv_sem=pass_recv.at[which, origin],
            device_id={"seq": here + flipped(bits)},
            device_id_type=MESH,
        )

    def mix_line(step, upward, origin):
        send, recv = (up_send, up_recv) if upward else (down_send, down_recv)
        block = mixes_ref.at[origin * group_size + member]
        return pltpu.make_async_remote_copy(
            src_ref=mix_ref if step == 1 else block,
            dst_ref=block,
            send_sem=send.at[step - 1, group_size],
            recv_sem=recv.at[step - 1, group_size],
            device_id={"seq": above if upward else below},
            device_id_type=MESH,
        )

    def pass_on(origin):
        mix_side(origin, 1, flipped(1), False).wait_recv()
        mix_pass(origin, flipped(1), 0, 2).start()
        mix_side(origin, 2, flipped(2), False).wait_recv()
        mix_pass(origin, flipped(2), 1, 1).start()

    def mix_step(step):
        for upward in (True, False):

            @pl.when(receives(step, upward))
            def _():
                origin = group - step if upward else group + step
                if step > 0:
                    mix_line(step, upward, origin).wait_recv()
                if step < groups - 1:

                    @pl.when(sends(step + 1, upward))
                    def _():
                        mix_line(step + 1, upward, origin).start()

                if step > 0 or upward:
                    mix_side(origin, 1, member, step == 0).start()
                    mix_side(origin, 2, member, step == 0).start()

        if step == 1:
            pass_on(group)
        elif step > 1:
            for upward in (True, False):

                @pl.when(receives(step - 1, upward))
                def _():
                    pass_on(group - step + 1 if upward else group + step - 1)

    def relay(step, d, upward):
        origin = group - step + 1 if upward else group + step - 1
        block = origin * group_size + lax.rem(member - d + group_size, group_size)
        send, recv = (up_send, up_recv) if upward else (down_send, down_recv)
        return pltpu.make_async_remote_copy(
            src_ref=weights_ref.at[block],
            dst_ref=weights_ref.at[block],
            send_sem=send.at[step - 1, d],
            recv_sem=recv.at[step - 1, d],
            device_id={"seq": above if upward else below},
            device_id_type=MESH,
        )

    def arrival(step, d, upward):
        origin = group - step if upward else group + step
        block = origin * group_size + lax.rem(member - d + group_size, group_size)
        send, recv = (up_send, up_recv) if upward else (down_send, down_recv)
        return pltpu.make_async_remote_copy(
            src_ref=weights_ref.at[block],
            dst_ref=weights_ref.at[block],
            send_sem=send.at[step - 1, d],
            recv_sem=recv.at[step - 1, d],
            device_id={"seq": above if upward else below},
            device_id_type=MESH,
        )

    def sends(step, upward):
        if upward:
            return (group < groups - 1) & (group - step + 1 >= 0)
        return (group > 0) & (group + step - 1 <= groups - 1)

    def receives(step, upward):
        return group - step >= 0 if upward else group + step <= groups - 1

    mix_step(0)
    for step in range(1, groups):
        for d in range(group_size):
            if step == 1:
                if d == 0:
                    for copy in own:
                        copy.wait()
                else:
                    for part in range(3):
                        origin = here + lax.rem(member - d + group_size, group_size)
                        pltpu.make_async_remote_copy(
                            src_ref=piece(part, member),
                            dst_ref=slot(origin, part),
                            send_sem=plane_send.at[d - 1, part],
                            recv_sem=plane_recv.at[d - 1, part],
                            device_id={"seq": origin},
                            device_id_type=MESH,
                        ).wait_recv()
            for upward in (True, False):
                if step > 1:

                    @pl.when(receives(step - 1, upward))
                    def _():
                        arrival(step - 1, d, upward).wait_recv()

                @pl.when(sends(step, upward))
                def _():
                    relay(step, d, upward).start()

        if step == 1:
            token_direct(1, flipped(1)).wait_recv()
            token_half(flipped(1), 0, 2).start()
            twin(0, core).start()
            token_direct(2, flipped(2)).wait_recv()
            token_half(flipped(2), 1, 1).start()
            twin(1, core).start()
        mix_step(step)
        if step == 1:
            token_half(flipped(3), 0, 2).wait_recv()
            twin(2, core).start()
            token_half(flipped(3), 1, 1).wait_recv()
            twin(3, core).start()

    for upward in (True, False):

        @pl.when(receives(groups - 1, upward))
        def _():
            pass_on(group - groups + 1 if upward else group + groups - 1)

    own_rows.wait()
    own_mix.wait()
    for copy in plane:
        copy.wait_send()
    for bits in (1, 2):
        token_direct(bits, member).wait_send()
    token_half(flipped(1), 0, 2).wait_send()
    token_half(flipped(2), 1, 1).wait_send()
    for index in range(4):
        twin(index, core).wait_send()
        twin(index, 1 - core).wait_recv()
    for origin in range(groups):
        mix_side(origin, 1, member, False).wait_send()
        mix_side(origin, 2, member, False).wait_send()
        mix_pass(origin, flipped(1), 0, 2).wait_send()
        mix_pass(origin, flipped(2), 1, 1).wait_send()
        mix_pass(origin, flipped(3), 0, 2).wait_recv()
        mix_pass(origin, flipped(3), 1, 1).wait_recv()
    for step in range(1, groups):
        for upward in (True, False):

            @pl.when(sends(step, upward))
            def _():
                mix_line(step, upward, group).wait_send()

    for step in range(1, groups):
        for d in range(group_size):
            for upward in (True, False):

                @pl.when(sends(step, upward))
                def _():
                    relay(step, d, upward).wait_send()

                if step == groups - 1:

                    @pl.when(receives(step, upward))
                    def _():
                        arrival(step, d, upward).wait_recv()


def gather(rows, query_weight, key_weight, value_weight, mix_weight, group_size):
    shards = lax.axis_size("seq")
    groups = shards // group_size
    depth = query_weight.shape[0]
    width = (query_weight.shape[1] + key_weight.shape[1] + value_weight.shape[1]) // group_size
    row_count, model_width = rows.shape
    halves = rows.reshape(2, row_count // 2, model_width)
    dma = pltpu.SemaphoreType.DMA
    anywhere = pl.BlockSpec(memory_space=pl.ANY)
    weights, tokens, mixes = pl.pallas_call(
        functools.partial(gather_kernel, groups, group_size),
        out_shape=(
            jax.ShapeDtypeStruct((shards, depth, width), jnp.bfloat16),
            jax.ShapeDtypeStruct((group_size,) + halves.shape, jnp.bfloat16),
            jax.ShapeDtypeStruct((shards,) + mix_weight.shape, jnp.bfloat16),
        ),
        in_specs=[anywhere] * 5,
        out_specs=(anywhere, anywhere, anywhere),
        scratch_shapes=[
            dma((5,)),
            dma((group_size - 1, 3)),
            dma((group_size - 1, 3)),
            dma((4,)),
            dma((4,)),
            dma((4,)),
            dma((4,)),
            dma((groups - 1, group_size + 1)),
            dma((groups - 1, group_size + 1)),
            dma((groups - 1, group_size + 1)),
            dma((groups - 1, group_size + 1)),
            dma((2, groups)),
            dma((2, groups)),
            dma((2, groups)),
            dma((2, groups)),
        ],
        compiler_params=pltpu.CompilerParams(collective_id=0, has_side_effects=True),
        name="gather",
    )(halves, query_weight, key_weight, value_weight, mix_weight)
    return (
        weights.reshape(shards * depth, width),
        tokens.reshape(-1, model_width),
        mixes.reshape(-1, mix_weight.shape[1]),
    )


def attend_kernel(
    groups, group_size, row_count, projected_ref, cosine_ref, sine_ref, out_ref,
    query_ref, window_ref, sent_ref, halo_send, halo_recv, send_sem, recv_sem,
):
    group, member, core = place(group_size)
    here = group * group_size
    shard = here + member
    above = shard + group_size
    below = shard - group_size
    barrier = pltpu.get_barrier_semaphore()
    for d in range(1, group_size):
        peer = here + lax.rem(member + d, group_size)
        pl.semaphore_signal(barrier, inc=1, device_id={"seq": peer}, device_id_type=MESH)

    @pl.when(group > 0)
    def _():
        pl.semaphore_signal(barrier, inc=1, device_id={"seq": below}, device_id_type=MESH)

    @pl.when(group < groups - 1)
    def _():
        pl.semaphore_signal(barrier, inc=1, device_id={"seq": above}, device_id_type=MESH)

    pl.semaphore_wait(
        barrier,
        group_size - 1 + jnp.where(group > 0, 1, 0) + jnp.where(group < groups - 1, 1, 0),
    )
    span = group_size * row_count
    query_width = query_ref.shape[1]
    query_heads = query_width // HEAD_DIM

    def rotated(block):
        scaled = block * lax.rsqrt(jnp.mean(block * block, axis=-1, keepdims=True) + NORM_EPS)
        turned = pltpu.roll(scaled, HEAD_DIM // 2, 1)
        return (scaled * cosine_ref[...] + turned * sine_ref[...]).astype(jnp.bfloat16)

    window_ref[pl.ds(span, span), :HEAD_DIM] = rotated(
        projected_ref[:, query_width : query_width + HEAD_DIM]
    )
    window_ref[pl.ds(span, span), HEAD_DIM:] = projected_ref[
        :, query_width + HEAD_DIM :
    ].astype(jnp.bfloat16)
    halo = pltpu.make_async_remote_copy(
        src_ref=window_ref.at[pl.ds(span, span)],
        dst_ref=window_ref.at[pl.ds(0, span)],
        send_sem=halo_send,
        recv_sem=halo_recv,
        device_id={"seq": above},
        device_id_type=MESH,
    )

    @pl.when(group < groups - 1)
    def _():
        halo.start()

    for head in range(query_heads):
        columns = slice(head * HEAD_DIM, (head + 1) * HEAD_DIM)
        query_ref[:, columns] = rotated(projected_ref[:, columns])

    @pl.when(group == 0)
    def _():
        window_ref[pl.ds(0, span), :] = jnp.zeros((span, window_ref.shape[1]), jnp.bfloat16)

    @pl.when(group > 0)
    def _():
        halo.wait_recv()

    reach = span + row_count
    query_pos = lax.broadcasted_iota(jnp.int32, (row_count, reach), 0) + span
    key_pos = lax.broadcasted_iota(jnp.int32, (row_count, reach), 1)
    distance = query_pos - key_pos
    near = (distance >= 0) & (distance < WINDOW)
    score_scale = 1.0 / math.sqrt(QSCALE)
    copies = []
    for turn in range(1, group_size + 1):
        index = lax.rem(member + turn, group_size)
        first = pl.multiple_of(index * row_count, row_count)
        keys = window_ref[pl.ds(first, reach), :HEAD_DIM]
        values = window_ref[pl.ds(first, reach), HEAD_DIM:]
        visible = near & (key_pos + first + group * span >= span)
        for head in range(query_heads):
            columns = slice(head * HEAD_DIM, (head + 1) * HEAD_DIM)
            scores = lax.dot_general(
                query_ref[pl.ds(first, row_count), columns], keys,
                (((1,), (1,)), ((), ())), preferred_element_type=jnp.float32,
            )
            raw = jnp.where(visible, jnp.exp(scores * score_scale), 0.0)
            probs = (raw * (1.0 / jnp.sum(raw, axis=-1, keepdims=True))).astype(jnp.bfloat16)
            sent_ref[turn - 1, :, columns] = jnp.dot(
                probs, values, preferred_element_type=jnp.float32
            ).astype(jnp.bfloat16)
        mine = out_ref.at[:, pl.ds(pl.multiple_of(member * query_width, query_width), query_width)]
        if turn < group_size:
            copy = pltpu.make_async_remote_copy(
                src_ref=sent_ref.at[turn - 1],
                dst_ref=mine,
                send_sem=send_sem.at[turn - 1],
                recv_sem=recv_sem.at[turn - 1],
                device_id={"seq": here + index},
                device_id_type=MESH,
            )
        else:
            copy = pltpu.make_async_copy(sent_ref.at[turn - 1], mine, send_sem.at[turn - 1])
        copy.start()
        copies.append(copy)
    copies[-1].wait()
    for turn in range(1, group_size):
        copies[turn - 1].wait_send()
        origin = lax.rem(member - turn + group_size, group_size)
        pltpu.make_async_remote_copy(
            src_ref=sent_ref.at[turn - 1],
            dst_ref=out_ref.at[
                :, pl.ds(pl.multiple_of(origin * query_width, query_width), query_width)
            ],
            send_sem=send_sem.at[turn - 1],
            recv_sem=recv_sem.at[turn - 1],
            device_id={"seq": here + origin},
            device_id_type=MESH,
        ).wait_recv()

    @pl.when(group < groups - 1)
    def _():
        halo.wait_send()


def attend(projected, cosine, sine, group_size):
    groups = lax.axis_size("seq") // group_size
    span = projected.shape[0]
    row_count = span // group_size
    query_width = projected.shape[1] - 2 * HEAD_DIM
    dma = pltpu.SemaphoreType.DMA
    vmem = pl.BlockSpec(memory_space=pltpu.VMEM)
    return pl.pallas_call(
        functools.partial(attend_kernel, groups, group_size, row_count),
        out_shape=jax.ShapeDtypeStruct((row_count, group_size * query_width), jnp.bfloat16),
        in_specs=[vmem] * 3,
        out_specs=vmem,
        scratch_shapes=[
            pltpu.VMEM((span, query_width), jnp.bfloat16),
            pltpu.VMEM((2 * span, 2 * HEAD_DIM), jnp.bfloat16),
            pltpu.VMEM((group_size, row_count, query_width), jnp.bfloat16),
            dma,
            dma,
            dma((group_size,)),
            dma((group_size - 1,)),
        ],
        compiler_params=pltpu.CompilerParams(
            collective_id=1, has_side_effects=True, vmem_limit_bytes=40 * 1024 * 1024
        ),
        name="attend",
    )(projected, cosine, sine)


def finish_kernel(
    partial_ref, residual_ref, gain_ref, out_ref, other_ref, total_ref, mine_ref, theirs_ref,
    send_sem, recv_sem,
):
    core = lax.axis_index("mp")
    barrier = pltpu.get_barrier_semaphore()
    pl.semaphore_signal(barrier, inc=1, device_id={"mp": 1 - core}, device_id_type=MESH)
    pl.semaphore_wait(barrier, 1)
    half = residual_ref.shape[1]

    def columns(index):
        return pl.ds(pl.multiple_of(index * half, 128), half)

    copy = pltpu.make_async_remote_copy(
        src_ref=partial_ref.at[:, columns(1 - core)],
        dst_ref=other_ref,
        send_sem=send_sem.at[0],
        recv_sem=recv_sem.at[0],
        device_id={"mp": 1 - core},
        device_id_type=MESH,
    )
    copy.start()
    copy.wait()
    total_ref[...] = partial_ref[:, columns(core)].astype(jnp.float32) + other_ref[...].astype(
        jnp.float32
    )
    squares = jnp.sum(total_ref[...] * total_ref[...], axis=1, keepdims=True)
    mine_ref[...] = jnp.broadcast_to(squares, mine_ref.shape)
    copy = pltpu.make_async_remote_copy(
        src_ref=mine_ref,
        dst_ref=theirs_ref,
        send_sem=send_sem.at[1],
        recv_sem=recv_sem.at[1],
        device_id={"mp": 1 - core},
        device_id_type=MESH,
    )
    copy.start()
    copy.wait()
    mean = (mine_ref[:, :1] + theirs_ref[:, :1]) / (2 * half)
    branch = total_ref[...] * lax.rsqrt(mean + NORM_EPS) * gain_ref[...]
    out_ref[...] = (residual_ref[...].astype(jnp.float32) + branch).astype(jnp.bfloat16)


def finish(partial_value, residual, gain):
    row_count, half = residual.shape
    dma = pltpu.SemaphoreType.DMA
    vmem = pl.BlockSpec(memory_space=pltpu.VMEM)
    return pl.pallas_call(
        finish_kernel,
        out_shape=jax.ShapeDtypeStruct((row_count, half), jnp.bfloat16),
        in_specs=[vmem] * 3,
        out_specs=vmem,
        scratch_shapes=[
            pltpu.VMEM((row_count, half), jnp.bfloat16),
            pltpu.VMEM((row_count, half), jnp.float32),
            pltpu.VMEM((row_count, 128), jnp.float32),
            pltpu.VMEM((row_count, 128), jnp.float32),
            dma((2,)),
            dma((2,)),
        ],
        compiler_params=pltpu.CompilerParams(
            collective_id=2, has_side_effects=True, vmem_limit_bytes=40 * 1024 * 1024
        ),
        name="finish",
    )(partial_value, residual, gain.reshape(1, half))


def body(hidden_in, query_weight, key_weight, value_weight, output_weight, input_gain, post_gain):
    row_count, model_width = hidden_in.shape
    half_width = post_gain.shape[1]
    core_index = lax.axis_index("mp")
    shard_index = lax.axis_index("seq")
    section_index = lax.axis_index("section")
    sections = lax.axis_size("section")
    shards = lax.axis_size("seq")
    group_size = key_weight.shape[2] // HEAD_DIM
    gain_first = input_gain[0].astype(jnp.float32)
    gain_second = post_gain[0].astype(jnp.float32)
    span = group_size * row_count
    positions = (shard_index // group_size) * span + jnp.arange(span, dtype=jnp.int32)
    cosine, sine = rope_tables(positions, HEAD_DIM)
    cosine = jnp.concatenate([cosine, cosine], axis=1)
    sine = jnp.concatenate([-sine, sine], axis=1)

    def normed_rows(full_rows):
        rows_float = full_rows.astype(jnp.float32)
        return (
            rows_float
            * lax.rsqrt(jnp.mean(rows_float * rows_float, axis=1, keepdims=True) + NORM_EPS)
            * gain_first
        ).astype(jnp.bfloat16)

    def attend_layer(weights, tokens, residual_half):
        projected = jnp.dot(tokens, weights, preferred_element_type=jnp.float32)
        attended = attend(projected, cosine, sine, group_size)
        partial_value = lax.dot_general(
            attended, mixes, (((1,), (1,)), ((), ())), preferred_element_type=jnp.float32
        ).astype(jnp.bfloat16)
        return finish(partial_value, residual_half, gain_second)

    own_half = lax.dynamic_slice_in_dim(hidden_in, core_index * half_width, half_width, 1)
    weights, tokens, mixes = gather(
        normed_rows(hidden_in),
        query_weight[0],
        key_weight[0],
        value_weight[0],
        output_weight[0].T,
        group_size,
    )
    layer = attend_layer(weights, tokens, own_half)
    result = layer
    plane = [
        list(range(first, first + group_size)) for first in range(0, shards, group_size)
    ]
    for step in range(1, sections):
        arrived = from_behind(layer, "section", 1)
        rows = normed_rows(lax.all_gather(arrived, "mp", axis=1, tiled=True))
        tokens = lax.all_gather(rows, "seq", axis=0, tiled=True, axis_index_groups=plane)
        layer = attend_layer(weights, tokens, arrived)
        result = jnp.where(section_index == step, layer, result)
    return result[None]


def solution(mesh):
    placed = (
        P("seq", None),
        P("section", "seq", "mp"),
        P("section", "seq", "mp"),
        P("section", "seq", "mp"),
        P("section", "mp", "seq"),
        P("section", None),
        P("section", "mp"),
    )
    return jax.shard_map(
        body, mesh=mesh, in_specs=placed, out_specs=P("section", "seq", "mp"), check_vma=False
    )
```

```python
import functools
import math

import jax
import jax.numpy as jnp
from jax import lax
from jax.experimental import pallas as pl
from jax.experimental.pallas import tpu as pltpu
from jax.sharding import PartitionSpec as P

HEADS = 16
KV_HEADS = 8
HEAD_DIM = 128
WINDOW = 1024
QSCALE = 168


NORM_EPS = 1e-06
MESH = pl.DeviceIdType.MESH


def from_behind(block, axis, distance):
    devices = range(lax.axis_size(axis))
    route = [(i - distance, i) for i in devices if i - distance in devices]
    return lax.ppermute(block, axis, route)


def rope_tables(positions, head_size):
    half_dim = head_size // 2
    frequency = jnp.exp(
        -math.log(10000.0) * (2.0 * jnp.arange(half_dim, dtype=jnp.float32)) / head_size
    )
    angles = positions.astype(jnp.float32)[:, None] * frequency[None, :]
    return (jnp.cos(angles), jnp.sin(angles))


def place(group_size):
    shard = lax.axis_index("seq")
    return lax.div(shard, group_size), lax.rem(shard, group_size), lax.axis_index("mp")


def gather_kernel(
    groups, group_size, hidden_ref, gain_ref, query_ref, key_ref, value_ref, mix_ref,
    weights_ref, tokens_ref, mixes_ref,
    own_sem, plane_send, plane_recv, token_send, token_recv, twin_send, twin_recv,
    up_send, up_recv, down_send, down_recv,
    side_send, side_recv, pass_send, pass_recv, rows_ref,
):
    group, member, core = place(group_size)
    here = group * group_size
    shard = here + member
    barrier = pltpu.get_barrier_semaphore()
    for d in range(1, group_size):
        peer = here + lax.rem(member + d, group_size)
        pl.semaphore_signal(barrier, inc=1, device_id={"seq": peer}, device_id_type=MESH)
    pl.semaphore_signal(barrier, inc=1, device_id={"mp": 1 - core}, device_id_type=MESH)
    above = shard + group_size
    below = shard - group_size

    @pl.when(group > 0)
    def _():
        pl.semaphore_signal(barrier, inc=1, device_id={"seq": below}, device_id_type=MESH)

    @pl.when(group < groups - 1)
    def _():
        pl.semaphore_signal(barrier, inc=1, device_id={"seq": above}, device_id_type=MESH)

    pl.semaphore_wait(
        barrier,
        group_size + jnp.where(group > 0, 1, 0) + jnp.where(group < groups - 1, 1, 0),
    )

    sources = (query_ref, key_ref, value_ref)
    widths = [ref.shape[1] // group_size for ref in sources]
    starts = [0, widths[0], widths[0] + widths[1]]

    def piece(part, index):
        width = widths[part]
        return sources[part].at[:, pl.ds(pl.multiple_of(index * width, width), width)]

    def slot(block, part):
        return weights_ref.at[block, :, pl.ds(starts[part], widths[part])]

    own = [
        pltpu.make_async_copy(piece(part, member), slot(shard, part), own_sem.at[part])
        for part in range(3)
    ]
    for copy in own:
        copy.start()
    plane = []
    for d in range(1, group_size):
        index = lax.rem(member + d, group_size)
        for part in range(3):
            copy = pltpu.make_async_remote_copy(
                src_ref=piece(part, index),
                dst_ref=slot(shard, part),
                send_sem=plane_send.at[d - 1, part],
                recv_sem=plane_recv.at[d - 1, part],
                device_id={"seq": here + index},
                device_id_type=MESH,
            )
            copy.start()
            plane.append(copy)
    own_mix = pltpu.make_async_copy(mix_ref, mixes_ref.at[shard], own_sem.at[4])
    own_mix.start()

    def flipped(bits):
        low = lax.rem(member, 2)
        high = member - low
        if bits & 1:
            low = 1 - low
        if bits & 2:
            high = 2 - high
        return high + low

    half_columns = rows_ref.shape[2] // 2

    def token_direct(bits, sender):
        return pltpu.make_async_remote_copy(
            src_ref=rows_ref.at[core],
            dst_ref=tokens_ref.at[sender, core],
            send_sem=token_send.at[bits - 1],
            recv_sem=token_recv.at[bits - 1],
            device_id={"seq": here + flipped(bits)},
            device_id_type=MESH,
        )

    def token_half(owner, which, bits):
        part = tokens_ref.at[owner, core, :, pl.ds(which * half_columns, half_columns)]
        return pltpu.make_async_remote_copy(
            src_ref=part,
            dst_ref=part,
            send_sem=token_send.at[2 + which],
            recv_sem=token_recv.at[2 + which],
            device_id={"seq": here + flipped(bits)},
            device_id_type=MESH,
        )

    def twin(index, half):
        if index < 2:
            part = tokens_ref.at[flipped(index + 1), half]
        else:
            part = tokens_ref.at[
                flipped(3), half, :, pl.ds((index - 2) * half_columns, half_columns)
            ]
        return pltpu.make_async_remote_copy(
            src_ref=part,
            dst_ref=part,
            send_sem=twin_send.at[index],
            recv_sem=twin_recv.at[index],
            device_id={"mp": 1 - core},
            device_id_type=MESH,
        )


    mix_half = mix_ref.shape[1] // 2

    def mix_side(origin, bits, owner, own):
        block = mixes_ref.at[origin * group_size + owner]
        return pltpu.make_async_remote_copy(
            src_ref=mix_ref if own else block,
            dst_ref=block,
            send_sem=side_send.at[bits - 1, origin],
            recv_sem=side_recv.at[bits - 1, origin],
            device_id={"seq": here + flipped(bits)},
            device_id_type=MESH,
        )

    def mix_pass(origin, owner, which, bits):
        part = mixes_ref.at[
            origin * group_size + owner, :, pl.ds(which * mix_half, mix_half)
        ]
        return pltpu.make_async_remote_copy(
            src_ref=part,
            dst_ref=part,
            send_sem=pass_send.at[which, origin],
            recv_sem=pass_recv.at[which, origin],
            device_id={"seq": here + flipped(bits)},
            device_id_type=MESH,
        )

    def mix_line(step, upward, origin):
        send, recv = (up_send, up_recv) if upward else (down_send, down_recv)
        block = mixes_ref.at[origin * group_size + member]
        return pltpu.make_async_remote_copy(
            src_ref=mix_ref if step == 1 else block,
            dst_ref=block,
            send_sem=send.at[step - 1, group_size],
            recv_sem=recv.at[step - 1, group_size],
            device_id={"seq": above if upward else below},
            device_id_type=MESH,
        )

    def pass_on(origin):
        mix_side(origin, 1, flipped(1), False).wait_recv()
        mix_pass(origin, flipped(1), 0, 2).start()
        mix_side(origin, 2, flipped(2), False).wait_recv()
        mix_pass(origin, flipped(2), 1, 1).start()

    def mix_step(step):
        for upward in (True, False):

            @pl.when(receives(step, upward))
            def _():
                origin = group - step if upward else group + step
                if step > 0:
                    mix_line(step, upward, origin).wait_recv()
                if step < groups - 1:

                    @pl.when(sends(step + 1, upward))
                    def _():
                        mix_line(step + 1, upward, origin).start()

                if step > 0 or upward:
                    mix_side(origin, 1, member, step == 0).start()
                    mix_side(origin, 2, member, step == 0).start()

        if step == 1:
            pass_on(group)
        elif step > 1:
            for upward in (True, False):

                @pl.when(receives(step - 1, upward))
                def _():
                    pass_on(group - step + 1 if upward else group + step - 1)

    def relay(step, d, upward):
        origin = group - step + 1 if upward else group + step - 1
        block = origin * group_size + lax.rem(member - d + group_size, group_size)
        send, recv = (up_send, up_recv) if upward else (down_send, down_recv)
        return pltpu.make_async_remote_copy(
            src_ref=weights_ref.at[block],
            dst_ref=weights_ref.at[block],
            send_sem=send.at[step - 1, d],
            recv_sem=recv.at[step - 1, d],
            device_id={"seq": above if upward else below},
            device_id_type=MESH,
        )

    def arrival(step, d, upward):
        origin = group - step if upward else group + step
        block = origin * group_size + lax.rem(member - d + group_size, group_size)
        send, recv = (up_send, up_recv) if upward else (down_send, down_recv)
        return pltpu.make_async_remote_copy(
            src_ref=weights_ref.at[block],
            dst_ref=weights_ref.at[block],
            send_sem=send.at[step - 1, d],
            recv_sem=recv.at[step - 1, d],
            device_id={"seq": above if upward else below},
            device_id_type=MESH,
        )

    def sends(step, upward):
        if upward:
            return (group < groups - 1) & (group - step + 1 >= 0)
        return (group > 0) & (group + step - 1 <= groups - 1)

    def receives(step, upward):
        return group - step >= 0 if upward else group + step <= groups - 1

    mix_step(0)
    chunk = 16
    for half in range(2):

        @pl.loop(0, rows_ref.shape[1] // chunk)
        def _(index):
            at = pl.ds(pl.multiple_of(index * chunk, chunk), chunk)
            values = hidden_ref[half, at, :].astype(jnp.float32)
            scale = lax.rsqrt(jnp.mean(values * values, axis=1, keepdims=True) + NORM_EPS)
            rows_ref[half, at, :] = (values * scale * gain_ref[...]).astype(jnp.bfloat16)

    token_direct(1, member).start()
    token_direct(2, member).start()
    own_rows = pltpu.make_async_copy(rows_ref, tokens_ref.at[member], own_sem.at[3])
    own_rows.start()
    for step in range(1, groups):
        for d in range(group_size):
            if step == 1:
                if d == 0:
                    for copy in own:
                        copy.wait()
                else:
                    for part in range(3):
                        origin = here + lax.rem(member - d + group_size, group_size)
                        pltpu.make_async_remote_copy(
                            src_ref=piece(part, member),
                            dst_ref=slot(origin, part),
                            send_sem=plane_send.at[d - 1, part],
                            recv_sem=plane_recv.at[d - 1, part],
                            device_id={"seq": origin},
                            device_id_type=MESH,
                        ).wait_recv()
            for upward in (True, False):
                if step > 1:

                    @pl.when(receives(step - 1, upward))
                    def _():
                        arrival(step - 1, d, upward).wait_recv()

                @pl.when(sends(step, upward))
                def _():
                    relay(step, d, upward).start()

        if step == 1:
            token_direct(1, flipped(1)).wait_recv()
            token_half(flipped(1), 0, 2).start()
            twin(0, core).start()
            token_direct(2, flipped(2)).wait_recv()
            token_half(flipped(2), 1, 1).start()
            twin(1, core).start()
        mix_step(step)
        if step == 1:
            token_half(flipped(3), 0, 2).wait_recv()
            twin(2, core).start()
            token_half(flipped(3), 1, 1).wait_recv()
            twin(3, core).start()

    for upward in (True, False):

        @pl.when(receives(groups - 1, upward))
        def _():
            pass_on(group - groups + 1 if upward else group + groups - 1)

    own_rows.wait()
    own_mix.wait()
    for copy in plane:
        copy.wait_send()
    for bits in (1, 2):
        token_direct(bits, member).wait_send()
    token_half(flipped(1), 0, 2).wait_send()
    token_half(flipped(2), 1, 1).wait_send()
    for index in range(4):
        twin(index, core).wait_send()
        twin(index, 1 - core).wait_recv()
    for origin in range(groups):
        mix_side(origin, 1, member, False).wait_send()
        mix_side(origin, 2, member, False).wait_send()
        mix_pass(origin, flipped(1), 0, 2).wait_send()
        mix_pass(origin, flipped(2), 1, 1).wait_send()
        mix_pass(origin, flipped(3), 0, 2).wait_recv()
        mix_pass(origin, flipped(3), 1, 1).wait_recv()
    for step in range(1, groups):
        for upward in (True, False):

            @pl.when(sends(step, upward))
            def _():
                mix_line(step, upward, group).wait_send()

    for step in range(1, groups):
        for d in range(group_size):
            for upward in (True, False):

                @pl.when(sends(step, upward))
                def _():
                    relay(step, d, upward).wait_send()

                if step == groups - 1:

                    @pl.when(receives(step, upward))
                    def _():
                        arrival(step, d, upward).wait_recv()


def gather(rows, gain, query_weight, key_weight, value_weight, mix_weight, group_size):
    shards = lax.axis_size("seq")
    groups = shards // group_size
    depth = query_weight.shape[0]
    width = (query_weight.shape[1] + key_weight.shape[1] + value_weight.shape[1]) // group_size
    row_count, model_width = rows.shape
    halves = rows.reshape(2, row_count // 2, model_width)
    dma = pltpu.SemaphoreType.DMA
    anywhere = pl.BlockSpec(memory_space=pl.ANY)
    weights, tokens, mixes = pl.pallas_call(
        functools.partial(gather_kernel, groups, group_size),
        out_shape=(
            jax.ShapeDtypeStruct((shards, depth, width), jnp.bfloat16),
            jax.ShapeDtypeStruct((group_size,) + halves.shape, jnp.bfloat16),
            jax.ShapeDtypeStruct((shards,) + mix_weight.shape, jnp.bfloat16),
        ),
        in_specs=[pl.BlockSpec(memory_space=pltpu.VMEM)] * 2 + [anywhere] * 4,
        out_specs=(anywhere, anywhere, anywhere),
        scratch_shapes=[
            dma((5,)),
            dma((group_size - 1, 3)),
            dma((group_size - 1, 3)),
            dma((4,)),
            dma((4,)),
            dma((4,)),
            dma((4,)),
            dma((groups - 1, group_size + 1)),
            dma((groups - 1, group_size + 1)),
            dma((groups - 1, group_size + 1)),
            dma((groups - 1, group_size + 1)),
            dma((2, groups)),
            dma((2, groups)),
            dma((2, groups)),
            dma((2, groups)),
            pltpu.VMEM(halves.shape, jnp.bfloat16),
        ],
        compiler_params=pltpu.CompilerParams(
            collective_id=0, has_side_effects=True, vmem_limit_bytes=32 * 1024 * 1024
        ),
        name="gather",
    )(halves, gain.reshape(1, model_width), query_weight, key_weight, value_weight, mix_weight)
    return (
        weights.reshape(shards * depth, width),
        tokens.reshape(-1, model_width),
        mixes.reshape(-1, mix_weight.shape[1]),
    )


def attend_kernel(
    groups, group_size, row_count, projected_ref, cosine_ref, sine_ref, mixes_ref, partial_ref,
    query_ref, window_ref, sent_ref, out_ref, held_ref,
    halo_send, halo_recv, send_sem, recv_sem, held_sem,
):
    group, member, core = place(group_size)
    here = group * group_size
    shard = here + member
    above = shard + group_size
    below = shard - group_size
    barrier = pltpu.get_barrier_semaphore()
    for d in range(1, group_size):
        peer = here + lax.rem(member + d, group_size)
        pl.semaphore_signal(barrier, inc=1, device_id={"seq": peer}, device_id_type=MESH)

    @pl.when(group > 0)
    def _():
        pl.semaphore_signal(barrier, inc=1, device_id={"seq": below}, device_id_type=MESH)

    @pl.when(group < groups - 1)
    def _():
        pl.semaphore_signal(barrier, inc=1, device_id={"seq": above}, device_id_type=MESH)

    pl.semaphore_wait(
        barrier,
        group_size - 1 + jnp.where(group > 0, 1, 0) + jnp.where(group < groups - 1, 1, 0),
    )
    held = pltpu.make_async_copy(mixes_ref, held_ref, held_sem)
    held.start()
    span = group_size * row_count
    query_width = query_ref.shape[1]
    query_heads = query_width // HEAD_DIM

    def rotated(block):
        scaled = block * lax.rsqrt(jnp.mean(block * block, axis=-1, keepdims=True) + NORM_EPS)
        turned = pltpu.roll(scaled, HEAD_DIM // 2, 1)
        return (scaled * cosine_ref[...] + turned * sine_ref[...]).astype(jnp.bfloat16)

    window_ref[pl.ds(span, span), :HEAD_DIM] = rotated(
        projected_ref[:, query_width : query_width + HEAD_DIM]
    )
    window_ref[pl.ds(span, span), HEAD_DIM:] = projected_ref[
        :, query_width + HEAD_DIM :
    ].astype(jnp.bfloat16)

    def halo(index):
        return pltpu.make_async_remote_copy(
            src_ref=window_ref.at[pl.ds(span + index * row_count, row_count)],
            dst_ref=window_ref.at[pl.ds(index * row_count, row_count)],
            send_sem=halo_send.at[index],
            recv_sem=halo_recv.at[index],
            device_id={"seq": above},
            device_id_type=MESH,
        )

    @pl.when(group < groups - 1)
    def _():
        for index in reversed(range(group_size)):
            halo(index).start()

    for head in range(query_heads):
        columns = slice(head * HEAD_DIM, (head + 1) * HEAD_DIM)
        query_ref[:, columns] = rotated(projected_ref[:, columns])

    @pl.when(group == 0)
    def _():
        window_ref[pl.ds(0, span), :] = jnp.zeros((span, window_ref.shape[1]), jnp.bfloat16)

    reach = span + row_count
    query_pos = lax.broadcasted_iota(jnp.int32, (row_count, reach), 0) + span
    key_pos = lax.broadcasted_iota(jnp.int32, (row_count, reach), 1)
    distance = query_pos - key_pos
    near = (distance >= 0) & (distance < WINDOW)
    score_scale = 1.0 / math.sqrt(QSCALE)

    def exchange(index, origin):
        return pltpu.make_async_remote_copy(
            src_ref=sent_ref.at[index],
            dst_ref=out_ref.at[
                :, pl.ds(pl.multiple_of(origin * query_width, query_width), query_width)
            ],
            send_sem=send_sem.at[index],
            recv_sem=recv_sem.at[origin],
            device_id={"seq": here + index},
            device_id_type=MESH,
        )

    own = pltpu.make_async_copy(
        sent_ref.at[member],
        out_ref.at[:, pl.ds(pl.multiple_of(member * query_width, query_width), query_width)],
        send_sem.at[member],
    )
    for index in reversed(range(group_size)):

        @pl.when(group > 0)
        def _():
            halo(index).wait_recv()

        first = index * row_count
        keys = window_ref[pl.ds(first, reach), :HEAD_DIM]
        values = window_ref[pl.ds(first, reach), HEAD_DIM:]
        visible = near & (key_pos + first + group * span >= span)
        for head in range(query_heads):
            columns = slice(head * HEAD_DIM, (head + 1) * HEAD_DIM)
            scores = lax.dot_general(
                query_ref[pl.ds(first, row_count), columns], keys,
                (((1,), (1,)), ((), ())), preferred_element_type=jnp.float32,
            )
            raw = jnp.where(visible, jnp.exp(scores * score_scale), 0.0)
            probs = (raw * (1.0 / jnp.sum(raw, axis=-1, keepdims=True))).astype(jnp.bfloat16)
            sent_ref[index, :, columns] = jnp.dot(
                probs, values, preferred_element_type=jnp.float32
            ).astype(jnp.bfloat16)

        @pl.when(member != index)
        def _():
            exchange(index, member).start()

        @pl.when(member == index)
        def _():
            own.start()

    for index in range(group_size):

        @pl.when(member != index)
        def _():
            exchange(index, member).wait_send()
            exchange(index, index).wait_recv()

        @pl.when(member == index)
        def _():
            own.wait()

    held.wait()
    tile = 384

    @pl.loop(0, partial_ref.shape[1] // tile)
    def _(index):
        at = pl.ds(pl.multiple_of(index * tile, tile), tile)
        partial_ref[:, at] = lax.dot_general(
            out_ref[...], held_ref[at, :], (((1,), (1,)), ((), ())),
            preferred_element_type=jnp.float32,
        ).astype(jnp.bfloat16)

    @pl.when(group < groups - 1)
    def _():
        for index in range(group_size):
            halo(index).wait_send()


def attend(projected, cosine, sine, mixes, group_size):
    groups = lax.axis_size("seq") // group_size
    span = projected.shape[0]
    row_count = span // group_size
    query_width = projected.shape[1] - 2 * HEAD_DIM
    dma = pltpu.SemaphoreType.DMA
    vmem = pl.BlockSpec(memory_space=pltpu.VMEM)
    return pl.pallas_call(
        functools.partial(attend_kernel, groups, group_size, row_count),
        out_shape=jax.ShapeDtypeStruct((row_count, mixes.shape[0]), jnp.bfloat16),
        in_specs=[vmem] * 3 + [pl.BlockSpec(memory_space=pl.ANY)],
        out_specs=vmem,
        scratch_shapes=[
            pltpu.VMEM((span, query_width), jnp.bfloat16),
            pltpu.VMEM((2 * span, 2 * HEAD_DIM), jnp.bfloat16),
            pltpu.VMEM((group_size, row_count, query_width), jnp.bfloat16),
            pltpu.VMEM((row_count, group_size * query_width), jnp.bfloat16),
            pltpu.VMEM(mixes.shape, jnp.bfloat16),
            dma((group_size,)),
            dma((group_size,)),
            dma((group_size,)),
            dma((group_size,)),
            dma,
        ],
        compiler_params=pltpu.CompilerParams(
            collective_id=1, has_side_effects=True, vmem_limit_bytes=40 * 1024 * 1024
        ),
        name="attend",
    )(projected, cosine, sine, mixes)


def finish_kernel(
    partial_ref, residual_ref, gain_ref, out_ref, other_ref, total_ref, mine_ref, theirs_ref,
    send_sem, recv_sem,
):
    core = lax.axis_index("mp")
    barrier = pltpu.get_barrier_semaphore()
    pl.semaphore_signal(barrier, inc=1, device_id={"mp": 1 - core}, device_id_type=MESH)
    pl.semaphore_wait(barrier, 1)
    half = residual_ref.shape[1]

    def columns(index):
        return pl.ds(pl.multiple_of(index * half, 128), half)

    copy = pltpu.make_async_remote_copy(
        src_ref=partial_ref.at[:, columns(1 - core)],
        dst_ref=other_ref,
        send_sem=send_sem.at[0],
        recv_sem=recv_sem.at[0],
        device_id={"mp": 1 - core},
        device_id_type=MESH,
    )
    copy.start()
    copy.wait()
    total_ref[...] = partial_ref[:, columns(core)].astype(jnp.float32) + other_ref[...].astype(
        jnp.float32
    )
    squares = jnp.sum(total_ref[...] * total_ref[...], axis=1, keepdims=True)
    mine_ref[...] = jnp.broadcast_to(squares, mine_ref.shape)
    copy = pltpu.make_async_remote_copy(
        src_ref=mine_ref,
        dst_ref=theirs_ref,
        send_sem=send_sem.at[1],
        recv_sem=recv_sem.at[1],
        device_id={"mp": 1 - core},
        device_id_type=MESH,
    )
    copy.start()
    copy.wait()
    mean = (mine_ref[:, :1] + theirs_ref[:, :1]) / (2 * half)
    branch = total_ref[...] * lax.rsqrt(mean + NORM_EPS) * gain_ref[...]
    out_ref[...] = (residual_ref[...].astype(jnp.float32) + branch).astype(jnp.bfloat16)


def finish(partial_value, residual, gain):
    row_count, half = residual.shape
    dma = pltpu.SemaphoreType.DMA
    vmem = pl.BlockSpec(memory_space=pltpu.VMEM)
    return pl.pallas_call(
        finish_kernel,
        out_shape=jax.ShapeDtypeStruct((row_count, half), jnp.bfloat16),
        in_specs=[vmem] * 3,
        out_specs=vmem,
        scratch_shapes=[
            pltpu.VMEM((row_count, half), jnp.bfloat16),
            pltpu.VMEM((row_count, half), jnp.float32),
            pltpu.VMEM((row_count, 128), jnp.float32),
            pltpu.VMEM((row_count, 128), jnp.float32),
            dma((2,)),
            dma((2,)),
        ],
        compiler_params=pltpu.CompilerParams(
            collective_id=2, has_side_effects=True, vmem_limit_bytes=40 * 1024 * 1024
        ),
        name="finish",
    )(partial_value, residual, gain.reshape(1, half))


def body(hidden_in, query_weight, key_weight, value_weight, output_weight, input_gain, post_gain):
    row_count, model_width = hidden_in.shape
    half_width = post_gain.shape[1]
    core_index = lax.axis_index("mp")
    shard_index = lax.axis_index("seq")
    section_index = lax.axis_index("section")
    sections = lax.axis_size("section")
    shards = lax.axis_size("seq")
    group_size = key_weight.shape[2] // HEAD_DIM
    gain_first = input_gain[0].astype(jnp.float32)
    gain_second = post_gain[0].astype(jnp.float32)
    span = group_size * row_count
    positions = (shard_index // group_size) * span + jnp.arange(span, dtype=jnp.int32)
    cosine, sine = rope_tables(positions, HEAD_DIM)
    cosine = jnp.concatenate([cosine, cosine], axis=1)
    sine = jnp.concatenate([-sine, sine], axis=1)

    def normed_rows(full_rows):
        rows_float = full_rows.astype(jnp.float32)
        return (
            rows_float
            * lax.rsqrt(jnp.mean(rows_float * rows_float, axis=1, keepdims=True) + NORM_EPS)
            * gain_first
        ).astype(jnp.bfloat16)

    def attend_layer(weights, tokens, residual_half):
        projected = jnp.dot(tokens, weights, preferred_element_type=jnp.float32)
        partial_value = attend(projected, cosine, sine, mixes, group_size)
        return finish(partial_value, residual_half, gain_second)

    own_half = lax.dynamic_slice_in_dim(hidden_in, core_index * half_width, half_width, 1)
    weights, tokens, mixes = gather(
        hidden_in,
        gain_first,
        query_weight[0],
        key_weight[0],
        value_weight[0],
        output_weight[0].T,
        group_size,
    )
    layer = attend_layer(weights, tokens, own_half)
    result = layer
    plane = [
        list(range(first, first + group_size)) for first in range(0, shards, group_size)
    ]
    for step in range(1, sections):
        arrived = from_behind(layer, "section", 1)
        rows = normed_rows(lax.all_gather(arrived, "mp", axis=1, tiled=True))
        tokens = lax.all_gather(rows, "seq", axis=0, tiled=True, axis_index_groups=plane)
        layer = attend_layer(weights, tokens, arrived)
        result = jnp.where(section_index == step, layer, result)
    return result[None]


def solution(mesh):
    placed = (
        P("seq", None),
        P("section", "seq", "mp"),
        P("section", "seq", "mp"),
        P("section", "seq", "mp"),
        P("section", "mp", "seq"),
        P("section", None),
        P("section", "mp"),
    )
    return jax.shard_map(
        body, mesh=mesh, in_specs=placed, out_specs=P("section", "seq", "mp"), check_vma=False
    )
```

```python
import functools
import math

import jax
import jax.numpy as jnp
from jax import lax
from jax.experimental import pallas as pl
from jax.experimental.pallas import tpu as pltpu
from jax.sharding import PartitionSpec as P

HEADS = 16
KV_HEADS = 8
HEAD_DIM = 128
WINDOW = 1024
QSCALE = 168


NORM_EPS = 1e-06
MESH = pl.DeviceIdType.MESH


def from_behind(block, axis, distance):
    devices = range(lax.axis_size(axis))
    route = [(i - distance, i) for i in devices if i - distance in devices]
    return lax.ppermute(block, axis, route)


def rope_tables(positions, head_size):
    half_dim = head_size // 2
    frequency = jnp.exp(
        -math.log(10000.0) * (2.0 * jnp.arange(half_dim, dtype=jnp.float32)) / head_size
    )
    angles = positions.astype(jnp.float32)[:, None] * frequency[None, :]
    return (jnp.cos(angles), jnp.sin(angles))


def place(group_size):
    shard = lax.axis_index("seq")
    return lax.div(shard, group_size), lax.rem(shard, group_size), lax.axis_index("mp")


def gather_kernel(
    groups, group_size, source_ref, gain_ref, query_ref, key_ref, value_ref, mix_ref,
    weights_ref, tokens_ref, mixes_ref,
    own_sem, plane_send, plane_recv, token_send, token_recv, twin_send, twin_recv,
    up_send, up_recv, down_send, down_recv,
    side_send, side_recv, pass_send, pass_recv, rows_ref, hidden_ref,
):
    group, member, core = place(group_size)
    here = group * group_size
    shard = here + member
    barrier = pltpu.get_barrier_semaphore()
    for d in range(1, group_size):
        peer = here + lax.rem(member + d, group_size)
        pl.semaphore_signal(barrier, inc=1, device_id={"seq": peer}, device_id_type=MESH)
    pl.semaphore_signal(barrier, inc=1, device_id={"mp": 1 - core}, device_id_type=MESH)
    above = shard + group_size
    below = shard - group_size

    @pl.when(group > 0)
    def _():
        pl.semaphore_signal(barrier, inc=1, device_id={"seq": below}, device_id_type=MESH)

    @pl.when(group < groups - 1)
    def _():
        pl.semaphore_signal(barrier, inc=1, device_id={"seq": above}, device_id_type=MESH)

    pl.semaphore_wait(
        barrier,
        group_size + jnp.where(group > 0, 1, 0) + jnp.where(group < groups - 1, 1, 0),
    )

    fetch = pltpu.make_async_copy(source_ref, hidden_ref, own_sem.at[5])
    fetch.start()
    sources = (query_ref, key_ref, value_ref)
    widths = [ref.shape[1] // group_size for ref in sources]
    starts = [0, widths[0], widths[0] + widths[1]]

    def piece(part, index):
        width = widths[part]
        return sources[part].at[:, pl.ds(pl.multiple_of(index * width, width), width)]

    def slot(block, part):
        return weights_ref.at[block, :, pl.ds(starts[part], widths[part])]

    own = [
        pltpu.make_async_copy(piece(part, member), slot(shard, part), own_sem.at[part])
        for part in range(3)
    ]
    for copy in own:
        copy.start()
    plane = []
    for d in range(1, group_size):
        index = lax.rem(member + d, group_size)
        for part in range(3):
            copy = pltpu.make_async_remote_copy(
                src_ref=piece(part, index),
                dst_ref=slot(shard, part),
                send_sem=plane_send.at[d - 1, part],
                recv_sem=plane_recv.at[d - 1, part],
                device_id={"seq": here + index},
                device_id_type=MESH,
            )
            copy.start()
            plane.append(copy)
    own_mix = pltpu.make_async_copy(mix_ref, mixes_ref.at[shard], own_sem.at[4])
    own_mix.start()

    def flipped(bits):
        low = lax.rem(member, 2)
        high = member - low
        if bits & 1:
            low = 1 - low
        if bits & 2:
            high = 2 - high
        return high + low

    half_columns = rows_ref.shape[2] // 2

    def token_direct(bits, sender):
        return pltpu.make_async_remote_copy(
            src_ref=rows_ref.at[core],
            dst_ref=tokens_ref.at[sender, core],
            send_sem=token_send.at[bits - 1],
            recv_sem=token_recv.at[bits - 1],
            device_id={"seq": here + flipped(bits)},
            device_id_type=MESH,
        )

    def token_half(owner, which, bits):
        part = tokens_ref.at[owner, core, :, pl.ds(which * half_columns, half_columns)]
        return pltpu.make_async_remote_copy(
            src_ref=part,
            dst_ref=part,
            send_sem=token_send.at[2 + which],
            recv_sem=token_recv.at[2 + which],
            device_id={"seq": here + flipped(bits)},
            device_id_type=MESH,
        )

    def twin(index, half):
        if index < 2:
            part = tokens_ref.at[flipped(index + 1), half]
        else:
            part = tokens_ref.at[
                flipped(3), half, :, pl.ds((index - 2) * half_columns, half_columns)
            ]
        return pltpu.make_async_remote_copy(
            src_ref=part,
            dst_ref=part,
            send_sem=twin_send.at[index],
            recv_sem=twin_recv.at[index],
            device_id={"mp": 1 - core},
            device_id_type=MESH,
        )


    mix_half = mix_ref.shape[1] // 2

    def mix_side(origin, bits, owner, own):
        block = mixes_ref.at[origin * group_size + owner]
        return pltpu.make_async_remote_copy(
            src_ref=mix_ref if own else block,
            dst_ref=block,
            send_sem=side_send.at[bits - 1, origin],
            recv_sem=side_recv.at[bits - 1, origin],
            device_id={"seq": here + flipped(bits)},
            device_id_type=MESH,
        )

    def mix_pass(origin, owner, which, bits):
        part = mixes_ref.at[
            origin * group_size + owner, :, pl.ds(which * mix_half, mix_half)
        ]
        return pltpu.make_async_remote_copy(
            src_ref=part,
            dst_ref=part,
            send_sem=pass_send.at[which, origin],
            recv_sem=pass_recv.at[which, origin],
            device_id={"seq": here + flipped(bits)},
            device_id_type=MESH,
        )

    def mix_line(step, upward, origin):
        send, recv = (up_send, up_recv) if upward else (down_send, down_recv)
        block = mixes_ref.at[origin * group_size + member]
        return pltpu.make_async_remote_copy(
            src_ref=mix_ref if step == 1 else block,
            dst_ref=block,
            send_sem=send.at[step - 1, group_size],
            recv_sem=recv.at[step - 1, group_size],
            device_id={"seq": above if upward else below},
            device_id_type=MESH,
        )

    def pass_on(origin):
        mix_side(origin, 1, flipped(1), False).wait_recv()
        mix_pass(origin, flipped(1), 0, 2).start()
        mix_side(origin, 2, flipped(2), False).wait_recv()
        mix_pass(origin, flipped(2), 1, 1).start()

    def mix_step(step):
        for upward in (True, False):

            @pl.when(receives(step, upward))
            def _():
                origin = group - step if upward else group + step
                if step > 0:
                    mix_line(step, upward, origin).wait_recv()
                if step < groups - 1:

                    @pl.when(sends(step + 1, upward))
                    def _():
                        mix_line(step + 1, upward, origin).start()

                if step > 0 or upward:
                    mix_side(origin, 1, member, step == 0).start()
                    mix_side(origin, 2, member, step == 0).start()

        if step == 1:
            pass_on(group)
        elif step > 1:
            for upward in (True, False):

                @pl.when(receives(step - 1, upward))
                def _():
                    pass_on(group - step + 1 if upward else group + step - 1)

    def relay(step, d, upward):
        origin = group - step + 1 if upward else group + step - 1
        block = origin * group_size + lax.rem(member - d + group_size, group_size)
        send, recv = (up_send, up_recv) if upward else (down_send, down_recv)
        return pltpu.make_async_remote_copy(
            src_ref=weights_ref.at[block],
            dst_ref=weights_ref.at[block],
            send_sem=send.at[step - 1, d],
            recv_sem=recv.at[step - 1, d],
            device_id={"seq": above if upward else below},
            device_id_type=MESH,
        )

    def arrival(step, d, upward):
        origin = group - step if upward else group + step
        block = origin * group_size + lax.rem(member - d + group_size, group_size)
        send, recv = (up_send, up_recv) if upward else (down_send, down_recv)
        return pltpu.make_async_remote_copy(
            src_ref=weights_ref.at[block],
            dst_ref=weights_ref.at[block],
            send_sem=send.at[step - 1, d],
            recv_sem=recv.at[step - 1, d],
            device_id={"seq": above if upward else below},
            device_id_type=MESH,
        )

    def sends(step, upward):
        if upward:
            return (group < groups - 1) & (group - step + 1 >= 0)
        return (group > 0) & (group + step - 1 <= groups - 1)

    def receives(step, upward):
        return group - step >= 0 if upward else group + step <= groups - 1

    mix_step(0)
    fetch.wait()
    chunk = 16
    for half in range(2):

        @pl.loop(0, rows_ref.shape[1] // chunk)
        def _(index):
            at = pl.ds(pl.multiple_of(index * chunk, chunk), chunk)
            values = hidden_ref[half, at, :].astype(jnp.float32)
            scale = lax.rsqrt(jnp.mean(values * values, axis=1, keepdims=True) + NORM_EPS)
            rows_ref[half, at, :] = (values * scale * gain_ref[...]).astype(jnp.bfloat16)

    token_direct(1, member).start()
    token_direct(2, member).start()
    own_rows = pltpu.make_async_copy(rows_ref, tokens_ref.at[member], own_sem.at[3])
    own_rows.start()
    for step in range(1, groups):
        for d in range(group_size):
            if step == 1:
                if d == 0:
                    for copy in own:
                        copy.wait()
                else:
                    for part in range(3):
                        origin = here + lax.rem(member - d + group_size, group_size)
                        pltpu.make_async_remote_copy(
                            src_ref=piece(part, member),
                            dst_ref=slot(origin, part),
                            send_sem=plane_send.at[d - 1, part],
                            recv_sem=plane_recv.at[d - 1, part],
                            device_id={"seq": origin},
                            device_id_type=MESH,
                        ).wait_recv()
            for upward in (True, False):
                if step > 1:

                    @pl.when(receives(step - 1, upward))
                    def _():
                        arrival(step - 1, d, upward).wait_recv()

                @pl.when(sends(step, upward))
                def _():
                    relay(step, d, upward).start()

        mix_step(step)
        if step == 1:
            token_direct(1, flipped(1)).wait_recv()
            token_half(flipped(1), 0, 2).start()
            twin(0, core).start()
            token_direct(2, flipped(2)).wait_recv()
            token_half(flipped(2), 1, 1).start()
            twin(1, core).start()
        if step == min(2, groups - 1):
            token_half(flipped(3), 0, 2).wait_recv()
            twin(2, core).start()
            token_half(flipped(3), 1, 1).wait_recv()
            twin(3, core).start()

    for upward in (True, False):

        @pl.when(receives(groups - 1, upward))
        def _():
            pass_on(group - groups + 1 if upward else group + groups - 1)

    own_rows.wait()
    own_mix.wait()
    for copy in plane:
        copy.wait_send()
    for bits in (1, 2):
        token_direct(bits, member).wait_send()
    token_half(flipped(1), 0, 2).wait_send()
    token_half(flipped(2), 1, 1).wait_send()
    for index in range(4):
        twin(index, core).wait_send()
        twin(index, 1 - core).wait_recv()
    for origin in range(groups):
        mix_side(origin, 1, member, False).wait_send()
        mix_side(origin, 2, member, False).wait_send()
        mix_pass(origin, flipped(1), 0, 2).wait_send()
        mix_pass(origin, flipped(2), 1, 1).wait_send()
        mix_pass(origin, flipped(3), 0, 2).wait_recv()
        mix_pass(origin, flipped(3), 1, 1).wait_recv()
    for step in range(1, groups):
        for upward in (True, False):

            @pl.when(sends(step, upward))
            def _():
                mix_line(step, upward, group).wait_send()

    for step in range(1, groups):
        for d in range(group_size):
            for upward in (True, False):

                @pl.when(sends(step, upward))
                def _():
                    relay(step, d, upward).wait_send()

                if step == groups - 1:

                    @pl.when(receives(step, upward))
                    def _():
                        arrival(step, d, upward).wait_recv()


def gather(rows, gain, query_weight, key_weight, value_weight, mix_weight, group_size):
    shards = lax.axis_size("seq")
    groups = shards // group_size
    depth = query_weight.shape[0]
    width = (query_weight.shape[1] + key_weight.shape[1] + value_weight.shape[1]) // group_size
    row_count, model_width = rows.shape
    halves = rows.reshape(2, row_count // 2, model_width)
    dma = pltpu.SemaphoreType.DMA
    anywhere = pl.BlockSpec(memory_space=pl.ANY)
    weights, tokens, mixes = pl.pallas_call(
        functools.partial(gather_kernel, groups, group_size),
        out_shape=(
            jax.ShapeDtypeStruct((shards, depth, width), jnp.bfloat16),
            jax.ShapeDtypeStruct((group_size,) + halves.shape, jnp.bfloat16),
            jax.ShapeDtypeStruct((shards,) + mix_weight.shape, jnp.bfloat16),
        ),
        in_specs=[anywhere, pl.BlockSpec(memory_space=pltpu.VMEM)] + [anywhere] * 4,
        out_specs=(anywhere, anywhere, anywhere),
        scratch_shapes=[
            dma((6,)),
            dma((group_size - 1, 3)),
            dma((group_size - 1, 3)),
            dma((4,)),
            dma((4,)),
            dma((4,)),
            dma((4,)),
            dma((groups - 1, group_size + 1)),
            dma((groups - 1, group_size + 1)),
            dma((groups - 1, group_size + 1)),
            dma((groups - 1, group_size + 1)),
            dma((2, groups)),
            dma((2, groups)),
            dma((2, groups)),
            dma((2, groups)),
            pltpu.VMEM(halves.shape, jnp.bfloat16),
            pltpu.VMEM(halves.shape, jnp.bfloat16),
        ],
        compiler_params=pltpu.CompilerParams(
            collective_id=0, has_side_effects=True, vmem_limit_bytes=32 * 1024 * 1024
        ),
        name="gather",
    )(halves, gain.reshape(1, model_width), query_weight, key_weight, value_weight, mix_weight)
    return (
        weights.reshape(shards * depth, width),
        tokens.reshape(-1, model_width),
        mixes.reshape(-1, mix_weight.shape[1]),
    )


def attend_kernel(
    groups, group_size, row_count, projected_ref, cosine_ref, sine_ref, mixes_ref, partial_ref,
    query_ref, window_ref, sent_ref, out_ref, held_ref,
    halo_send, halo_recv, send_sem, recv_sem, held_sem,
):
    group, member, core = place(group_size)
    here = group * group_size
    shard = here + member
    above = shard + group_size
    below = shard - group_size
    barrier = pltpu.get_barrier_semaphore()
    for d in range(1, group_size):
        peer = here + lax.rem(member + d, group_size)
        pl.semaphore_signal(barrier, inc=1, device_id={"seq": peer}, device_id_type=MESH)

    @pl.when(group > 0)
    def _():
        pl.semaphore_signal(barrier, inc=1, device_id={"seq": below}, device_id_type=MESH)

    @pl.when(group < groups - 1)
    def _():
        pl.semaphore_signal(barrier, inc=1, device_id={"seq": above}, device_id_type=MESH)

    pl.semaphore_wait(
        barrier,
        group_size - 1 + jnp.where(group > 0, 1, 0) + jnp.where(group < groups - 1, 1, 0),
    )
    held = pltpu.make_async_copy(mixes_ref, held_ref, held_sem)
    held.start()
    span = group_size * row_count
    query_width = query_ref.shape[1]
    query_heads = query_width // HEAD_DIM

    def rotated(block):
        scaled = block * lax.rsqrt(jnp.mean(block * block, axis=-1, keepdims=True) + NORM_EPS)
        turned = pltpu.roll(scaled, HEAD_DIM // 2, 1)
        return (scaled * cosine_ref[...] + turned * sine_ref[...]).astype(jnp.bfloat16)

    window_ref[pl.ds(span, span), :HEAD_DIM] = rotated(
        projected_ref[:, query_width : query_width + HEAD_DIM]
    )
    window_ref[pl.ds(span, span), HEAD_DIM:] = projected_ref[
        :, query_width + HEAD_DIM :
    ].astype(jnp.bfloat16)

    def halo(index):
        return pltpu.make_async_remote_copy(
            src_ref=window_ref.at[pl.ds(span + index * row_count, row_count)],
            dst_ref=window_ref.at[pl.ds(index * row_count, row_count)],
            send_sem=halo_send.at[index],
            recv_sem=halo_recv.at[index],
            device_id={"seq": above},
            device_id_type=MESH,
        )

    @pl.when(group < groups - 1)
    def _():
        for index in reversed(range(group_size)):
            halo(index).start()

    for head in range(query_heads):
        columns = slice(head * HEAD_DIM, (head + 1) * HEAD_DIM)
        query_ref[:, columns] = rotated(projected_ref[:, columns])

    @pl.when(group == 0)
    def _():
        window_ref[pl.ds(0, span), :] = jnp.zeros((span, window_ref.shape[1]), jnp.bfloat16)

    reach = span + row_count
    query_pos = lax.broadcasted_iota(jnp.int32, (row_count, reach), 0) + span
    key_pos = lax.broadcasted_iota(jnp.int32, (row_count, reach), 1)
    distance = query_pos - key_pos
    near = (distance >= 0) & (distance < WINDOW)
    score_scale = 1.0 / math.sqrt(QSCALE)

    def exchange(index, origin):
        return pltpu.make_async_remote_copy(
            src_ref=sent_ref.at[index],
            dst_ref=out_ref.at[
                :, pl.ds(pl.multiple_of(origin * query_width, query_width), query_width)
            ],
            send_sem=send_sem.at[index],
            recv_sem=recv_sem.at[origin],
            device_id={"seq": here + index},
            device_id_type=MESH,
        )

    own = pltpu.make_async_copy(
        sent_ref.at[member],
        out_ref.at[:, pl.ds(pl.multiple_of(member * query_width, query_width), query_width)],
        send_sem.at[member],
    )
    for index in reversed(range(group_size)):

        @pl.when(group > 0)
        def _():
            halo(index).wait_recv()

        first = index * row_count
        keys = window_ref[pl.ds(first, reach), :HEAD_DIM]
        values = window_ref[pl.ds(first, reach), HEAD_DIM:]
        visible = near & (key_pos + first + group * span >= span)
        for head in range(query_heads):
            columns = slice(head * HEAD_DIM, (head + 1) * HEAD_DIM)
            scores = lax.dot_general(
                query_ref[pl.ds(first, row_count), columns], keys,
                (((1,), (1,)), ((), ())), preferred_element_type=jnp.float32,
            )
            raw = jnp.where(visible, jnp.exp(scores * score_scale), 0.0)
            probs = (raw * (1.0 / jnp.sum(raw, axis=-1, keepdims=True))).astype(jnp.bfloat16)
            sent_ref[index, :, columns] = jnp.dot(
                probs, values, preferred_element_type=jnp.float32
            ).astype(jnp.bfloat16)

        @pl.when(member != index)
        def _():
            exchange(index, member).start()

        @pl.when(member == index)
        def _():
            own.start()

    for index in range(group_size):

        @pl.when(member != index)
        def _():
            exchange(index, member).wait_send()
            exchange(index, index).wait_recv()

        @pl.when(member == index)
        def _():
            own.wait()

    held.wait()
    tile = 384

    @pl.loop(0, partial_ref.shape[1] // tile)
    def _(index):
        at = pl.ds(pl.multiple_of(index * tile, tile), tile)
        partial_ref[:, at] = lax.dot_general(
            out_ref[...], held_ref[at, :], (((1,), (1,)), ((), ())),
            preferred_element_type=jnp.float32,
        ).astype(jnp.bfloat16)

    @pl.when(group < groups - 1)
    def _():
        for index in range(group_size):
            halo(index).wait_send()


def attend(projected, cosine, sine, mixes, group_size):
    groups = lax.axis_size("seq") // group_size
    span = projected.shape[0]
    row_count = span // group_size
    query_width = projected.shape[1] - 2 * HEAD_DIM
    dma = pltpu.SemaphoreType.DMA
    vmem = pl.BlockSpec(memory_space=pltpu.VMEM)
    return pl.pallas_call(
        functools.partial(attend_kernel, groups, group_size, row_count),
        out_shape=jax.ShapeDtypeStruct((row_count, mixes.shape[0]), jnp.bfloat16),
        in_specs=[vmem] * 3 + [pl.BlockSpec(memory_space=pl.ANY)],
        out_specs=vmem,
        scratch_shapes=[
            pltpu.VMEM((span, query_width), jnp.bfloat16),
            pltpu.VMEM((2 * span, 2 * HEAD_DIM), jnp.bfloat16),
            pltpu.VMEM((group_size, row_count, query_width), jnp.bfloat16),
            pltpu.VMEM((row_count, group_size * query_width), jnp.bfloat16),
            pltpu.VMEM(mixes.shape, jnp.bfloat16),
            dma((group_size,)),
            dma((group_size,)),
            dma((group_size,)),
            dma((group_size,)),
            dma,
        ],
        compiler_params=pltpu.CompilerParams(
            collective_id=1, has_side_effects=True, vmem_limit_bytes=40 * 1024 * 1024
        ),
        name="attend",
    )(projected, cosine, sine, mixes)


def finish_kernel(
    partial_ref, residual_ref, gain_ref, out_ref, other_ref, total_ref, mine_ref, theirs_ref,
    send_sem, recv_sem,
):
    core = lax.axis_index("mp")
    barrier = pltpu.get_barrier_semaphore()
    pl.semaphore_signal(barrier, inc=1, device_id={"mp": 1 - core}, device_id_type=MESH)
    pl.semaphore_wait(barrier, 1)
    half = residual_ref.shape[1]

    def columns(index):
        return pl.ds(pl.multiple_of(index * half, 128), half)

    copy = pltpu.make_async_remote_copy(
        src_ref=partial_ref.at[:, columns(1 - core)],
        dst_ref=other_ref,
        send_sem=send_sem.at[0],
        recv_sem=recv_sem.at[0],
        device_id={"mp": 1 - core},
        device_id_type=MESH,
    )
    copy.start()
    copy.wait()
    total_ref[...] = partial_ref[:, columns(core)].astype(jnp.float32) + other_ref[...].astype(
        jnp.float32
    )
    squares = jnp.sum(total_ref[...] * total_ref[...], axis=1, keepdims=True)
    mine_ref[...] = jnp.broadcast_to(squares, mine_ref.shape)
    copy = pltpu.make_async_remote_copy(
        src_ref=mine_ref,
        dst_ref=theirs_ref,
        send_sem=send_sem.at[1],
        recv_sem=recv_sem.at[1],
        device_id={"mp": 1 - core},
        device_id_type=MESH,
    )
    copy.start()
    copy.wait()
    mean = (mine_ref[:, :1] + theirs_ref[:, :1]) / (2 * half)
    branch = total_ref[...] * lax.rsqrt(mean + NORM_EPS) * gain_ref[...]
    out_ref[...] = (residual_ref[...].astype(jnp.float32) + branch).astype(jnp.bfloat16)


def finish(partial_value, residual, gain):
    row_count, half = residual.shape
    dma = pltpu.SemaphoreType.DMA
    vmem = pl.BlockSpec(memory_space=pltpu.VMEM)
    return pl.pallas_call(
        finish_kernel,
        out_shape=jax.ShapeDtypeStruct((row_count, half), jnp.bfloat16),
        in_specs=[vmem] * 3,
        out_specs=vmem,
        scratch_shapes=[
            pltpu.VMEM((row_count, half), jnp.bfloat16),
            pltpu.VMEM((row_count, half), jnp.float32),
            pltpu.VMEM((row_count, 128), jnp.float32),
            pltpu.VMEM((row_count, 128), jnp.float32),
            dma((2,)),
            dma((2,)),
        ],
        compiler_params=pltpu.CompilerParams(
            collective_id=2, has_side_effects=True, vmem_limit_bytes=40 * 1024 * 1024
        ),
        name="finish",
    )(partial_value, residual, gain.reshape(1, half))


def body(hidden_in, query_weight, key_weight, value_weight, output_weight, input_gain, post_gain):
    row_count, model_width = hidden_in.shape
    half_width = post_gain.shape[1]
    core_index = lax.axis_index("mp")
    shard_index = lax.axis_index("seq")
    section_index = lax.axis_index("section")
    sections = lax.axis_size("section")
    shards = lax.axis_size("seq")
    group_size = key_weight.shape[2] // HEAD_DIM
    gain_first = input_gain[0].astype(jnp.float32)
    gain_second = post_gain[0].astype(jnp.float32)
    span = group_size * row_count
    positions = (shard_index // group_size) * span + jnp.arange(span, dtype=jnp.int32)
    cosine, sine = rope_tables(positions, HEAD_DIM)
    cosine = jnp.concatenate([cosine, cosine], axis=1)
    sine = jnp.concatenate([-sine, sine], axis=1)

    def normed_rows(full_rows):
        rows_float = full_rows.astype(jnp.float32)
        return (
            rows_float
            * lax.rsqrt(jnp.mean(rows_float * rows_float, axis=1, keepdims=True) + NORM_EPS)
            * gain_first
        ).astype(jnp.bfloat16)

    def attend_layer(weights, tokens, residual_half):
        projected = jnp.dot(tokens, weights, preferred_element_type=jnp.float32)
        partial_value = attend(projected, cosine, sine, mixes, group_size)
        return finish(partial_value, residual_half, gain_second)

    own_half = lax.dynamic_slice_in_dim(hidden_in, core_index * half_width, half_width, 1)
    weights, tokens, mixes = gather(
        hidden_in,
        gain_first,
        query_weight[0],
        key_weight[0],
        value_weight[0],
        output_weight[0].T,
        group_size,
    )
    layer = attend_layer(weights, tokens, own_half)
    result = layer
    plane = [
        list(range(first, first + group_size)) for first in range(0, shards, group_size)
    ]
    for step in range(1, sections):
        arrived = from_behind(layer, "section", 1)
        rows = normed_rows(lax.all_gather(arrived, "mp", axis=1, tiled=True))
        tokens = lax.all_gather(rows, "seq", axis=0, tiled=True, axis_index_groups=plane)
        layer = attend_layer(weights, tokens, arrived)
        result = jnp.where(section_index == step, layer, result)
    return result[None]


def solution(mesh):
    placed = (
        P("seq", None),
        P("section", "seq", "mp"),
        P("section", "seq", "mp"),
        P("section", "seq", "mp"),
        P("section", "mp", "seq"),
        P("section", None),
        P("section", "mp"),
    )
    return jax.shard_map(
        body, mesh=mesh, in_specs=placed, out_specs=P("section", "seq", "mp"), check_vma=False
    )
```
